512 devices in a mesh: rep: 16 (over x, y), fsdp: 32 (over z, core).
Axes of the slice: x: 4, y: 4, z: 16, core: 2. Of those that a mesh axis runs over, the one named last changes fastest.
Arguments:
- grad_parts: bfloat16 [16, 48, 512, 512], P('rep', None, 'fsdp'), may hold values from -2 to 2
- momentum: float32 [96, 512, 512], P('rep', 'fsdp'), may hold values from -160 to 160
- weight: float32 [48, 512, 512], P(None, 'fsdp'), may hold values from -0.25 to 0.25
- owners: int32 [48], replicated, may hold values from 0 to 15, as said below
Outputs:
- step_update: float32 [48, 512, 512], P(None, 'fsdp')
- new_weight: float32 [48, 512, 512], P(None, 'fsdp')
- new_momentum: float32 [96, 512, 512], P('rep', 'fsdp')
The draws below stay inside these ranges and needn't reach their ends.
Inputs may be any that keep to these rules, and one draw needn't show every extreme that they name: `owners`: each block names one replica group. No group owns more than 6 blocks, and one group owns exactly 6.
All inputs are finite; a program needn't handle non-finite values.
Results may differ from the reference program's by a relative error of at most 0.025.
Values may be sent and summed in bfloat16 or wider, within the bound.
No kernel may reach another device: no remote copies, remote signals or barrier semaphores. Data moves between devices by JAX's collectives and lax.ppermute only.
A program may use at most 64 MiB of HBM per device.

```python
import math
import jax
import jax.numpy as jnp
from jax import lax

BLK = 512
NBLK = 48
NS_ITERS = 3
MOST = 6
SLOTS = 96
N_REP = 16


def draw_owners(key, part):
    key = jax.random.fold_in(key, 11)
    first_key, second_key = jax.random.split(key)
    owner_order = jax.random.permutation(first_key, N_REP).astype(jnp.int32)
    block_ids = jnp.arange(NBLK, dtype=jnp.int32)
    others = (1 + (block_ids - MOST) % (N_REP - 1)).astype(jnp.int32)
    base_owner = jnp.where(block_ids < MOST, 0, others).astype(jnp.int32)
    shuffle = jax.random.permutation(second_key, NBLK).astype(jnp.int32)
    return owner_order[base_owner[shuffle]].astype(jnp.int32)


def draw_momentum(key, part):
    key = jax.random.fold_in(key, 5)
    noise_key, row_key, col_key = jax.random.split(key, 3)
    noise_field = jax.random.normal(noise_key, (SLOTS, BLK, BLK), jnp.float32)
    spread = math.log(10.0)
    row_scale = jnp.exp(jax.random.uniform(row_key, (SLOTS, BLK, 1), jnp.float32, 0.0, spread))
    col_scale = jnp.exp(jax.random.uniform(col_key, (SLOTS, 1, BLK), jnp.float32, 0.0, spread))
    return jnp.clip(0.1 * noise_field * row_scale * col_scale, -160.0, 160.0).astype(jnp.float32)


def strengthened(values, own_key, source, target, blocks, factor):
    owner, partner = [(jnp.arange(values.shape[dim]) // (values.shape[dim] // blocks)).reshape([-1 if axis == dim else 1 for axis in range(values.ndim)]) for dim in (source, target)]
    chosen = jax.random.permutation(own_key, blocks)[partner]
    strong = (owner == chosen) | (owner == (partner + blocks // 2) % blocks)
    return jnp.where(strong, factor * values, values)


def block_scale(rng, shape, pieces, low, top_value):
    factor_of = 1.0
    for dim, parts in pieces:
        heights = jax.random.uniform(jax.random.fold_in(jax.random.fold_in(rng, 6), dim), (parts,), jnp.float32, low / len(pieces), top_value / len(pieces))
        factor_of = factor_of * jnp.repeat(jnp.exp(heights), shape[dim] // parts).reshape((-1,) + (1,) * (len(shape) - 1 - dim))
    return factor_of


def centred(rng, dims, scale, limit, cuts=(), kind=jnp.bfloat16):
    factor_of = block_scale(rng, dims, cuts, -0.22, 0.18) if cuts else 1.0
    drawn = jax.random.normal(rng, dims, jnp.float32) * scale * factor_of
    return jnp.minimum(jnp.maximum(drawn, -limit), limit).astype(kind)


def heavy_noise(rng, extent, deviation, reach, pieces, heavy, held_as=jnp.bfloat16):
    drawn = deviation * jax.random.normal(rng, extent, jnp.float32)
    if pieces:
        drawn = drawn * block_scale(rng, extent, pieces, -0.22, 0.18)
    return jnp.clip(strengthened(drawn, jax.random.fold_in(rng, 3), *heavy), -reach, reach).astype(held_as)


def setup_inputs(seed: int = 0) -> dict:
    key_of = jax.random.split(jax.random.key(seed), 5)
    return {
        "grad_parts": heavy_noise(key_of[0], (N_REP, NBLK, BLK, BLK), 0.25, 2.0, ((0, 16), (2, 32)), (0, 1, 16, 2.0)),
        "momentum": draw_momentum(jax.random.fold_in(key_of[4], 71), 0),
        "weight": centred(key_of[2], (NBLK, BLK, BLK), BLK ** -0.5, 0.25, ((1, 32),), jnp.float32),
        "owners": draw_owners(jax.random.fold_in(key_of[4], 71), 0),
    }


COEF_A = 3.4445
COEF_B = -4.775
COEF_C = 2.0315
MOMENTUM_DECAY = 0.95
LEARN_RATE = 0.02
EPSILON = 1e-07

def orthogonalize(direction):
    rounded = direction.astype(jnp.bfloat16)
    widened = lax.optimization_barrier(rounded).astype(jnp.float32)
    frobenius = jnp.sqrt(jnp.sum(widened * widened))
    current = (widened / (frobenius + EPSILON)).astype(jnp.bfloat16)
    for iteration in range(NS_ITERS):
        gram_matrix = jnp.dot(current, current.T, preferred_element_type=jnp.float32).astype(jnp.bfloat16)
        square = jnp.dot(gram_matrix, gram_matrix, preferred_element_type=jnp.float32)
        polynomial = (COEF_B * gram_matrix.astype(jnp.float32) + COEF_C * square).astype(jnp.bfloat16)
        current = (COEF_A * current.astype(jnp.float32) + jnp.dot(polynomial, current, preferred_element_type=jnp.float32)).astype(jnp.bfloat16)
    return current

def accumulate(running, portion):
    return (running + portion.astype(jnp.float32), None)

def reference(grad_parts, momentum, weight, owners):
    gradient = lax.scan(accumulate, jnp.zeros(grad_parts.shape[1:], jnp.float32), grad_parts)[0]
    positions = jnp.arange(NBLK, dtype=jnp.int32)
    matching = (owners[None, :] == owners[:, None]) & (positions[None, :] < positions[:, None])
    slot_index = lax.optimization_barrier(jnp.sum(matching.astype(jnp.int32), axis=1)).astype(jnp.int32)
    location = (owners * MOST + slot_index).astype(jnp.int32)
    new_momentum = momentum
    updates = []
    for block_id in range(NBLK):
        previous = momentum[location[block_id]]
        advanced = MOMENTUM_DECAY * previous + gradient[block_id]
        new_momentum = new_momentum.at[location[block_id]].set(advanced)
        direction = gradient[block_id] + MOMENTUM_DECAY * advanced
        updates.append(orthogonalize(direction).astype(jnp.float32) * (0.2 * math.sqrt(BLK)))
    step_update = jnp.stack(updates)
    new_weight = weight - LEARN_RATE * step_update
    return (step_update, new_weight, new_momentum)
```

```python
import functools
import math

import jax
import jax.numpy as jnp
from jax import lax
from jax.experimental import pallas as pl
from jax.experimental.pallas import tpu as pltpu
from jax.sharding import PartitionSpec as P

NS_ITERS = 3
COEF_A = 3.4445
COEF_B = -4.775
COEF_C = 2.0315
MOMENTUM_DECAY = 0.95
LEARN_RATE = 0.02
EPSILON = 1e-07
DIRECTION_SCALE = 1.0 + MOMENTUM_DECAY
FOLD = MOMENTUM_DECAY * MOMENTUM_DECAY / DIRECTION_SCALE
SEGMENT = 4

VMEM = pl.BlockSpec(memory_space=pltpu.VMEM)
SMEM = pl.BlockSpec(memory_space=pltpu.SMEM)


def folded(part, momentum):
    return (part.astype(jnp.float32) + FOLD * momentum).astype(jnp.bfloat16)


def for_owned(owners_ref, here_ref, body):
    here = here_ref[0]

    def step(block, slot):
        mine = owners_ref[block] == here

        @pl.when(mine)
        def _():
            body(block, slot)

        return slot + mine.astype(jnp.int32)

    lax.fori_loop(0, owners_ref.shape[0], step, jnp.int32(0))


def fold_kernel(owners_ref, here_ref, part_ref, momentum_ref, out_ref):
    out_ref[...] = part_ref[...]

    def body(block, slot):
        out_ref[block] = folded(part_ref[block], momentum_ref[slot])

    for_owned(owners_ref, here_ref, body)


def momentum_kernel(owners_ref, here_ref, total_ref, part_ref, momentum_ref, out_ref):
    out_ref[...] = momentum_ref[...]

    def body(block, slot):
        part = part_ref[block].astype(jnp.float32)
        old = momentum_ref[slot]
        added = folded(part_ref[block], old).astype(jnp.float32) - part
        gradient = total_ref[block].astype(jnp.float32) - added
        out_ref[slot] = MOMENTUM_DECAY * old + gradient

    for_owned(owners_ref, here_ref, body)


def sum_kernel(parts_ref, send_ref, total_ref):
    count, blocks = parts_ref.shape[:2]
    for block in range(blocks):
        total = parts_ref[0, block].astype(jnp.float32)
        for source in range(1, count):
            total = total + parts_ref[source, block].astype(jnp.float32)
        total_ref[block] = total.astype(jnp.bfloat16)
        direction = (DIRECTION_SCALE * total).astype(jnp.bfloat16)
        for target in range(send_ref.shape[0]):
            if min(target % SEGMENT, blocks - 1) == block:
                send_ref[target] = direction


def dot_nt(a, b):
    return lax.dot_general(a, b, (((1,), (1,)), ((), ())), preferred_element_type=jnp.float32)


def dot_nn(a, b):
    return jnp.dot(a, b, preferred_element_type=jnp.float32)


def newton_schulz_kernel(segment_ref, own_ref, other_ref, out_ref, x_ref, gram_ref, poly_ref):
    half, order = own_ref.shape
    kept = out_ref.shape[0]
    squares = jnp.float32(0.0)
    for ref in (own_ref, other_ref):
        wide = ref[...].astype(jnp.float32)
        squares = squares + jnp.sum(wide * wide)
    inverse = 1.0 / (jnp.sqrt(squares) + EPSILON)
    x_ref[0:half] = (own_ref[...].astype(jnp.float32) * inverse).astype(jnp.bfloat16)
    x_ref[half:order] = (other_ref[...].astype(jnp.float32) * inverse).astype(jnp.bfloat16)
    tiles = [pl.ds(start, half) for start in range(0, order, half)]
    for iteration in range(NS_ITERS):
        for rows in tiles:
            gram_ref[rows] = dot_nt(x_ref[rows], x_ref[...]).astype(jnp.bfloat16)
        if iteration == NS_ITERS - 1:
            rows = pl.ds(pl.multiple_of(segment_ref[0] * kept, kept), kept)
            gram = gram_ref[rows]
            poly = (COEF_B * gram.astype(jnp.float32) + COEF_C * dot_nn(gram, gram_ref[...])).astype(jnp.bfloat16)
            out_ref[...] = (
                COEF_A * x_ref[rows].astype(jnp.float32) + dot_nn(poly, x_ref[...])
            ).astype(jnp.bfloat16)
            return
        for rows in tiles:
            gram = gram_ref[rows]
            poly_ref[rows] = (
                COEF_B * gram.astype(jnp.float32) + COEF_C * dot_nn(gram, gram_ref[...])
            ).astype(jnp.bfloat16)
        fresh = [
            (COEF_A * x_ref[rows].astype(jnp.float32) + dot_nn(poly_ref[rows], x_ref[...])).astype(jnp.bfloat16)
            for rows in tiles
        ]
        for rows, value in zip(tiles, fresh):
            x_ref[rows] = value


def call(kernel, out_shape, in_specs, scratch=(), flops=0, moved=0):
    return pl.pallas_call(
        kernel,
        out_shape=out_shape,
        in_specs=in_specs,
        out_specs=jax.tree.map(lambda _: VMEM, out_shape),
        scratch_shapes=list(scratch),
        compiler_params=pltpu.CompilerParams(vmem_limit_bytes=24 * 1024 * 1024),
        cost_estimate=pl.CostEstimate(flops=flops, bytes_accessed=moved, transcendentals=0),
    )


def on_device(grad_parts, momentum, weight, owners):
    part = grad_parts[0]
    blocks, rows, order = part.shape
    groups = lax.axis_size("rep")
    members = lax.axis_size("fsdp")
    chips = members // 2
    per_group = blocks // groups
    bf16 = functools.partial(jax.ShapeDtypeStruct, dtype=jnp.bfloat16)
    here = lax.axis_index("rep").astype(jnp.int32).reshape(1)
    segment = (lax.axis_index("fsdp") // (2 * SEGMENT)).astype(jnp.int32).reshape(1)
    same_core = [[2 * chip + core for chip in range(chips)] for core in range(2)]
    same_segment = [
        [2 * (SEGMENT * s + chip) + core for chip in range(SEGMENT)]
        for s in range(chips // SEGMENT)
        for core in range(2)
    ]

    with jax.named_scope("fold_momentum"):
        folded_parts = call(
            fold_kernel, bf16((blocks, rows, order)), [SMEM, SMEM, VMEM, VMEM], moved=1 << 21
        )(owners, here, part, momentum)
    with jax.named_scope("reduce_over_rep"):
        received = lax.all_to_all(
            folded_parts.reshape(groups, per_group, rows, order), "rep", 0, 0, tiled=True
        )
        send, total = call(
            sum_kernel,
            [bf16((chips, rows, order)), bf16((per_group, rows, order))],
            [VMEM],
            moved=1 << 20,
        )(received)
    with jax.named_scope("gather_rows"):
        own = lax.all_to_all(send, "fsdp", 0, 0, axis_index_groups=same_core, tiled=True)
        own = own.reshape(chips * rows, order)
        other = lax.ppermute(own, "fsdp", [(i, i ^ 1) for i in range(members)])
    with jax.named_scope("orthogonalize"):
        square = pltpu.VMEM((order, order), jnp.bfloat16)
        kept = call(
            newton_schulz_kernel,
            bf16((SEGMENT * rows, order)),
            [SMEM, VMEM, VMEM],
            [square] * 3,
            flops=15 * order**3,
            moved=1 << 20,
        )(segment, own, other)
    with jax.named_scope("return_rows"):
        returned = lax.all_to_all(
            kept.reshape(SEGMENT, rows, order), "fsdp", 0, 0, axis_index_groups=same_segment, tiled=True
        )[:per_group]
        collected = lax.all_to_all(
            jnp.broadcast_to(returned[None], (groups, per_group, rows, order)), "rep", 0, 0, tiled=True
        ).reshape(blocks, rows, order)
    with jax.named_scope("update_weight"):
        step_update = collected.astype(jnp.float32) * (0.2 * math.sqrt(order))
        new_weight = weight - LEARN_RATE * step_update
    with jax.named_scope("update_momentum"):
        totals = lax.all_to_all(
            jnp.broadcast_to(total[None], (groups, per_group, rows, order)), "rep", 0, 0, tiled=True
        ).reshape(blocks, rows, order)
        new_momentum = call(
            momentum_kernel,
            jax.ShapeDtypeStruct(momentum.shape, jnp.float32),
            [SMEM, SMEM, VMEM, VMEM, VMEM],
            moved=1 << 21,
        )(owners, here, totals, part, momentum)
    return (step_update, new_weight, new_momentum)


def solution(mesh):
    return jax.shard_map(
        on_device,
        mesh=mesh,
        in_specs=(P("rep", None, "fsdp", None), P("rep", "fsdp", None), P(None, "fsdp", None), P()),
        out_specs=(P(None, "fsdp", None), P(None, "fsdp", None), P("rep", "fsdp", None)),
        check_vma=False,
    )
```

```python
import functools
import math

import jax
import jax.numpy as jnp
from jax import lax
from jax.experimental import pallas as pl
from jax.experimental.pallas import tpu as pltpu
from jax.sharding import PartitionSpec as P

NS_ITERS = 3
COEF_A = 3.4445
COEF_B = -4.775
COEF_C = 2.0315
MOMENTUM_DECAY = 0.95
LEARN_RATE = 0.02
EPSILON = 1e-07
DIRECTION_SCALE = 1.0 + MOMENTUM_DECAY
FOLD = MOMENTUM_DECAY * MOMENTUM_DECAY / DIRECTION_SCALE
SEGMENT = 4
PIECES = 6

VMEM = pl.BlockSpec(memory_space=pltpu.VMEM)
SMEM = pl.BlockSpec(memory_space=pltpu.SMEM)
HBM = pl.BlockSpec(memory_space=pltpu.HBM)


class Table:
    def __init__(self, blocks, most, per_group):
        self.block = 0
        self.own_from = blocks
        self.own_block = self.own_from + most
        self.held_owner = self.own_block + most
        self.count = self.held_owner + per_group
        self.unused = self.count + 1
        self.size = 128


def folded(part, momentum):
    return (part.astype(jnp.float32) + FOLD * momentum).astype(jnp.bfloat16)


def fold_kernel(
    table,
    groups,
    here_ref,
    owners_hbm,
    part_hbm,
    momentum_hbm,
    out_hbm,
    table_ref,
    owners_ref,
    count_ref,
    slot_ref,
    part_ref,
    momentum_ref,
    sems,
):
    blocks, most = part_ref.shape[0], momentum_ref.shape[0]
    per_group = blocks // groups
    copies = [
        pltpu.make_async_copy(source, target, sems.at[index])
        for index, (source, target) in enumerate(
            [(owners_hbm, owners_ref), (part_hbm, part_ref), (momentum_hbm, momentum_ref)]
        )
    ]
    for copy in copies:
        copy.start()
    here = here_ref[0]
    for group in range(groups):
        count_ref[group] = 0
    copies[0].wait()
    for block in range(blocks):
        owner = owners_ref[block]
        slot = count_ref[owner]
        slot_ref[block] = slot
        count_ref[owner] = slot + 1
    table_ref[table.count] = count_ref[here]
    first = jnp.int32(0)
    for group in range(groups):
        after = first + count_ref[group]
        count_ref[group] = first
        first = after
    for block in range(blocks):
        owner, slot = owners_ref[block], slot_ref[block]
        rank = count_ref[owner] + slot
        group, place = rank & (groups - 1), rank >> (groups.bit_length() - 1)
        where = group * SEGMENT + place
        table_ref[table.block + block] = where
        mine = owner == here
        table_ref[jnp.where(mine, table.own_from + slot, table.unused)] = where
        table_ref[jnp.where(mine, table.own_block + slot, table.unused)] = block
        table_ref[jnp.where(group == here, table.held_owner + place, table.unused)] = owner
    for copy in copies[1:]:
        copy.wait()
    for slot in range(most):

        @pl.when(slot < table_ref[table.count])
        def _():
            block = table_ref[table.own_block + slot]
            part_ref[block] = folded(part_ref[block], momentum_ref[slot])

    for block in range(blocks):
        where = table_ref[table.block + block]
        target = (where // SEGMENT) * per_group + (where & (SEGMENT - 1))
        pltpu.make_async_copy(part_ref.at[block], out_hbm.at[target], sems.at[3]).start()
    pltpu.make_async_copy(part_ref, out_hbm, sems.at[3]).wait()


def sum_kernel(parts_ref, send_ref, total_ref):
    count, blocks = parts_ref.shape[:2]
    for block in range(blocks):
        total = parts_ref[0, block].astype(jnp.float32)
        for source in range(1, count):
            total = total + parts_ref[source, block].astype(jnp.float32)
        total_ref[block] = total.astype(jnp.bfloat16)
        direction = (DIRECTION_SCALE * total).astype(jnp.bfloat16)
        for target in range(send_ref.shape[0]):
            if min(target % SEGMENT, blocks - 1) == block:
                send_ref[target] = direction


def dot_nt(a, b):
    return lax.dot_general(a, b, (((1,), (1,)), ((), ())), preferred_element_type=jnp.float32)


def dot_nn(a, b):
    return jnp.dot(a, b, preferred_element_type=jnp.float32)


def newton_schulz_kernel(segment_ref, own_ref, other_ref, out_ref, x_ref, gram_ref, poly_ref):
    half, order = own_ref.shape
    kept = out_ref.shape[0]
    squares = jnp.float32(0.0)
    for ref in (own_ref, other_ref):
        wide = ref[...].astype(jnp.float32)
        squares = squares + jnp.sum(wide * wide)
    inverse = 1.0 / (jnp.sqrt(squares) + EPSILON)
    x_ref[0:half] = (own_ref[...].astype(jnp.float32) * inverse).astype(jnp.bfloat16)
    x_ref[half:order] = (other_ref[...].astype(jnp.float32) * inverse).astype(jnp.bfloat16)
    tiles = [pl.ds(start, half) for start in range(0, order, half)]
    for iteration in range(NS_ITERS):
        for rows in tiles:
            gram_ref[rows] = dot_nt(x_ref[rows], x_ref[...]).astype(jnp.bfloat16)
        if iteration == NS_ITERS - 1:
            rows = pl.ds(pl.multiple_of(segment_ref[0] * kept, kept), kept)
            gram = gram_ref[rows]
            poly = (COEF_B * gram.astype(jnp.float32) + COEF_C * dot_nn(gram, gram_ref[...])).astype(jnp.bfloat16)
            out_ref[...] = (
                COEF_A * x_ref[rows].astype(jnp.float32) + dot_nn(poly, x_ref[...])
            ).astype(jnp.bfloat16)
            return
        for rows in tiles:
            gram = gram_ref[rows]
            poly_ref[rows] = (
                COEF_B * gram.astype(jnp.float32) + COEF_C * dot_nn(gram, gram_ref[...])
            ).astype(jnp.bfloat16)
        fresh = [
            (COEF_A * x_ref[rows].astype(jnp.float32) + dot_nn(poly_ref[rows], x_ref[...])).astype(jnp.bfloat16)
            for rows in tiles
        ]
        for rows, value in zip(tiles, fresh):
            x_ref[rows] = value


def spread_kernel(table, table_ref, returned_ref, total_ref, out_ref):
    per_group = total_ref.shape[0]
    for place in range(per_group):
        value = returned_ref[place]
        for target in range(out_ref.shape[0]):
            out_ref[target, place] = value
    for target in range(out_ref.shape[0]):
        out_ref[target, per_group] = total_ref[0]
    for place in range(per_group):
        out_ref[table_ref[table.held_owner + place], per_group] = total_ref[place]


def update_kernel(
    table,
    scale,
    table_ref,
    both_ref,
    weight_hbm,
    part_hbm,
    momentum_hbm,
    step_hbm,
    new_hbm,
    moved_hbm,
    weight_ref,
    part_ref,
    momentum_ref,
    step_ref,
    new_ref,
    moved_ref,
    sems,
    slot_sems,
):
    blocks, most = weight_ref.shape[0], momentum_ref.shape[0]
    each = blocks // PIECES
    chunks = [pl.ds(index * each, each) for index in range(PIECES)]
    arriving = [
        pltpu.make_async_copy(weight_hbm.at[chunk], weight_ref.at[chunk], sems.at[index, 0])
        for index, chunk in enumerate(chunks)
    ]
    old = pltpu.make_async_copy(momentum_hbm, momentum_ref, sems.at[PIECES, 0])
    count = table_ref[table.count]
    parts = [
        pltpu.make_async_copy(
            part_hbm.at[jnp.where(slot < count, table_ref[table.own_block + slot], 0)],
            part_ref.at[slot],
            slot_sems.at[slot],
        )
        for slot in range(most)
    ]
    for copy in arriving + [old] + parts:
        copy.start()
    leaving = []

    def leave(source, target, sem):
        leaving.append(pltpu.make_async_copy(source, target, sem))
        leaving[-1].start()

    for index, chunk in enumerate(chunks):
        for block in range(index * each, (index + 1) * each):
            step_ref[block] = both_ref[table_ref[table.block + block]].astype(jnp.float32) * scale
        leave(step_ref.at[chunk], step_hbm.at[chunk], sems.at[index, 1])
    for index, chunk in enumerate(chunks):
        arriving[index].wait()
        new_ref[chunk] = weight_ref[chunk] - LEARN_RATE * step_ref[chunk]
        leave(new_ref.at[chunk], new_hbm.at[chunk], sems.at[index, 2])
    old.wait()
    for slot in range(most):
        parts[slot].wait()
        part = part_ref[slot]
        before = momentum_ref[slot]
        added = folded(part, before).astype(jnp.float32) - part.astype(jnp.float32)
        used = slot < count
        source = jnp.where(used, table_ref[table.own_from + slot], 0) | (SEGMENT - 1)
        gradient = both_ref[source].astype(jnp.float32) - added
        moved_ref[slot] = jnp.where(used, MOMENTUM_DECAY * before + gradient, before)
    leave(moved_ref, moved_hbm, sems.at[PIECES, 1])
    for copy in leaving:
        copy.wait()


def call(kernel, out_shape, in_specs, scratch=(), flops=0, moved=0, out_specs=None, room=40.0):
    return pl.pallas_call(
        kernel,
        out_shape=out_shape,
        in_specs=in_specs,
        out_specs=jax.tree.map(lambda _: VMEM, out_shape) if out_specs is None else out_specs,
        scratch_shapes=list(scratch),
        compiler_params=pltpu.CompilerParams(vmem_limit_bytes=int((64 - room) * 1024 * 1024)),
        cost_estimate=pl.CostEstimate(flops=flops, bytes_accessed=moved, transcendentals=0),
    )


def on_device(grad_parts, momentum, weight, owners):
    part = grad_parts[0]
    blocks, rows, order = part.shape
    most = momentum.shape[0]
    groups = lax.axis_size("rep")
    members = lax.axis_size("fsdp")
    chips = members // 2
    per_group = blocks // groups
    table = Table(blocks, most, per_group)
    bf16 = functools.partial(jax.ShapeDtypeStruct, dtype=jnp.bfloat16)
    f32 = functools.partial(jax.ShapeDtypeStruct, dtype=jnp.float32)
    here = lax.axis_index("rep").astype(jnp.int32).reshape(1)
    segment = (lax.axis_index("fsdp") // (2 * SEGMENT)).astype(jnp.int32).reshape(1)
    same_core = [[2 * chip + core for chip in range(chips)] for core in range(2)]
    same_segment = [
        [2 * (SEGMENT * s + chip) + core for chip in range(SEGMENT)]
        for s in range(chips // SEGMENT)
        for core in range(2)
    ]

    with jax.named_scope("fold_momentum"):
        parts, places = call(
            functools.partial(fold_kernel, table, groups),
            [bf16((blocks, rows, order)), jax.ShapeDtypeStruct((table.size,), jnp.int32)],
            [SMEM, HBM, HBM, HBM],
            [
                pltpu.SMEM((blocks,), jnp.int32),
                pltpu.SMEM((groups,), jnp.int32),
                pltpu.SMEM((blocks,), jnp.int32),
                pltpu.VMEM(part.shape, jnp.bfloat16),
                pltpu.VMEM(momentum.shape, jnp.float32),
                pltpu.SemaphoreType.DMA((4,)),
            ],
            moved=1 << 21,
            out_specs=[HBM, SMEM],
            room=1,
        )(here, owners, part, momentum)
    with jax.named_scope("reduce_over_rep"):
        received = lax.all_to_all(
            parts.reshape(groups, per_group, rows, order), "rep", 0, 0, tiled=True
        )
        send, total = call(
            sum_kernel,
            [bf16((chips, rows, order)), bf16((per_group, rows, order))],
            [VMEM],
            moved=1 << 20,
        )(received)
    with jax.named_scope("gather_rows"):
        own = lax.all_to_all(send, "fsdp", 0, 0, axis_index_groups=same_core, tiled=True)
        own = own.reshape(chips * rows, order)
        other = lax.ppermute(own, "fsdp", [(i, i ^ 1) for i in range(members)])
    with jax.named_scope("orthogonalize"):
        square = pltpu.VMEM((order, order), jnp.bfloat16)
        kept = call(
            newton_schulz_kernel,
            bf16((SEGMENT * rows, order)),
            [SMEM, VMEM, VMEM],
            [square] * 3,
            flops=15 * order**3,
            moved=1 << 20,
        )(segment, own, other)
    with jax.named_scope("return_rows"):
        returned = lax.all_to_all(
            kept.reshape(SEGMENT, rows, order), "fsdp", 0, 0, axis_index_groups=same_segment, tiled=True
        )
        spread = call(
            functools.partial(spread_kernel, table),
            bf16((groups, SEGMENT, rows, order)),
            [SMEM, VMEM, VMEM],
            moved=1 << 20,
        )(places, returned, total)
        both = lax.all_to_all(spread, "rep", 0, 0, tiled=True).reshape(groups * SEGMENT, rows, order)
    with jax.named_scope("update"):
        return call(
            functools.partial(update_kernel, table, 0.2 * math.sqrt(order)),
            [f32(weight.shape), f32(weight.shape), f32(momentum.shape)],
            [SMEM, VMEM, HBM, HBM, HBM],
            [
                pltpu.VMEM(weight.shape, jnp.float32),
                pltpu.VMEM((most, rows, order), jnp.bfloat16),
                pltpu.VMEM(momentum.shape, jnp.float32),
                pltpu.VMEM(weight.shape, jnp.float32),
                pltpu.VMEM(weight.shape, jnp.float32),
                pltpu.VMEM(momentum.shape, jnp.float32),
                pltpu.SemaphoreType.DMA((PIECES + 1, 3)),
                pltpu.SemaphoreType.DMA((most,)),
            ],
            moved=5 << 20,
            out_specs=[HBM, HBM, HBM],
            room=3,
        )(places, both, weight, part, momentum)


def solution(mesh):
    return jax.shard_map(
        on_device,
        mesh=mesh,
        in_specs=(P("rep", None, "fsdp", None), P("rep", "fsdp", None), P(None, "fsdp", None), P()),
        out_specs=(P(None, "fsdp", None), P(None, "fsdp", None), P("rep", "fsdp", None)),
        check_vma=False,
    )
```

```python
import functools
import math

import jax
import jax.numpy as jnp
from jax import lax
from jax.experimental import pallas as pl
from jax.experimental.pallas import tpu as pltpu
from jax.sharding import PartitionSpec as P

NS_ITERS = 3
COEF_A = 3.4445
COEF_B = -4.775
COEF_C = 2.0315
MOMENTUM_DECAY = 0.95
LEARN_RATE = 0.02
EPSILON = 1e-07
DIRECTION_SCALE = 1.0 + MOMENTUM_DECAY
FOLD = MOMENTUM_DECAY * MOMENTUM_DECAY / DIRECTION_SCALE
SEGMENT = 4
PIECES = 6

VMEM = pl.BlockSpec(memory_space=pltpu.VMEM)
SMEM = pl.BlockSpec(memory_space=pltpu.SMEM)
HBM = pl.BlockSpec(memory_space=pltpu.HBM)
ANY = pl.BlockSpec(memory_space=pl.ANY)


class Table:
    def __init__(self, blocks, most, per_group):
        self.block = 0
        self.own_from = blocks
        self.own_block = self.own_from + most
        self.held_owner = self.own_block + most
        self.count = self.held_owner + per_group
        self.unused = self.count + 1
        self.size = 128


def folded(part, momentum):
    return (part.astype(jnp.float32) + FOLD * momentum).astype(jnp.bfloat16)


def fold_kernel(
    table,
    groups,
    here_ref,
    owners_hbm,
    part_hbm,
    momentum_hbm,
    out_hbm,
    table_hbm,
    table_ref,
    owners_ref,
    count_ref,
    slot_ref,
    part_ref,
    momentum_ref,
    sems,
):
    blocks, most = part_ref.shape[0], momentum_ref.shape[0]
    per_group = blocks // groups
    copies = [
        pltpu.make_async_copy(source, target, sems.at[index])
        for index, (source, target) in enumerate(
            [(owners_hbm, owners_ref), (part_hbm, part_ref), (momentum_hbm, momentum_ref)]
        )
    ]
    for copy in copies:
        copy.start()
    here = here_ref[0]
    for group in range(groups):
        count_ref[group] = 0
    copies[0].wait()
    for block in range(blocks):
        owner = owners_ref[block]
        slot = count_ref[owner]
        slot_ref[block] = slot
        count_ref[owner] = slot + 1
    used = count_ref[here]
    table_ref[table.count] = used
    first = jnp.int32(0)
    for group in range(groups):
        after = first + count_ref[group]
        count_ref[group] = first
        first = after
    copies[1].wait()
    for block in range(blocks):
        owner, slot = owners_ref[block], slot_ref[block]
        rank = count_ref[owner] + slot
        group, place = rank & (groups - 1), rank >> (groups.bit_length() - 1)
        where = group * SEGMENT + place
        table_ref[table.block + block] = where
        mine = owner == here
        table_ref[jnp.where(mine, table.own_from + slot, table.unused)] = where
        table_ref[jnp.where(mine, table.own_block + slot, table.unused)] = block
        table_ref[jnp.where(group == here, table.held_owner + place, table.unused)] = owner

        @pl.when(jnp.logical_not(mine))
        def _():
            target = group * per_group + place
            pltpu.make_async_copy(part_ref.at[block], out_hbm.at[target], sems.at[3]).start()

    table_out = pltpu.make_async_copy(table_ref, table_hbm, sems.at[4])
    table_out.start()
    copies[2].wait()
    for slot in range(most):

        @pl.when(slot < used)
        def _():
            block = table_ref[table.own_block + slot]
            where = table_ref[table.own_from + slot]
            target = (where >> (SEGMENT.bit_length() - 1)) * per_group + (where & (SEGMENT - 1))
            part_ref[block] = folded(part_ref[block], momentum_ref[slot])
            pltpu.make_async_copy(part_ref.at[block], out_hbm.at[target], sems.at[3]).start()

    pltpu.make_async_copy(part_ref, out_hbm, sems.at[3]).wait()
    table_out.wait()


def sum_kernel(parts_ref, send_ref, total_ref):
    count, blocks = parts_ref.shape[:2]
    for block in range(blocks):
        total = parts_ref[0, block].astype(jnp.float32)
        for source in range(1, count):
            total = total + parts_ref[source, block].astype(jnp.float32)
        total_ref[block] = total.astype(jnp.bfloat16)
        direction = (DIRECTION_SCALE * total).astype(jnp.bfloat16)
        for target in range(send_ref.shape[0]):
            if min(target % SEGMENT, blocks - 1) == block:
                send_ref[target] = direction


def dot_nt(a, b):
    return lax.dot_general(a, b, (((1,), (1,)), ((), ())), preferred_element_type=jnp.float32)


def dot_nn(a, b):
    return jnp.dot(a, b, preferred_element_type=jnp.float32)


def newton_schulz_kernel(segment_ref, own_ref, other_ref, out_ref, x_ref, y_ref, gram_ref, poly_ref):
    half, order = own_ref.shape
    kept = out_ref.shape[0]
    x_ref[0:half] = own_ref[...]
    x_ref[half:order] = other_ref[...]
    squares = jnp.zeros((8, order), jnp.float32)
    for ref in (own_ref, other_ref):
        wide = ref[...].astype(jnp.float32)
        squares = squares + jnp.sum((wide * wide).reshape(half // 8, 8, order), axis=0)
    inverse = 1.0 / (jnp.sqrt(jnp.sum(squares)) + EPSILON)
    source_ref, target_ref = x_ref, y_ref
    for iteration in range(NS_ITERS):
        gram = dot_nt(source_ref[...], source_ref[...])
        if iteration == 0:
            gram = gram * (inverse * inverse)
        gram_ref[...] = gram.astype(jnp.bfloat16)
        last = iteration == NS_ITERS - 1
        rows = pl.ds(pl.multiple_of(segment_ref[0] * kept, kept), kept) if last else pl.ds(0, order)
        gram = gram_ref[rows]
        poly = (COEF_B * gram.astype(jnp.float32) + COEF_C * dot_nn(gram, gram_ref[...])).astype(jnp.bfloat16)
        if not last:
            poly_ref[...] = poly
            poly = poly_ref[...]
        fresh = COEF_A * source_ref[rows].astype(jnp.float32) + dot_nn(poly, source_ref[...])
        if iteration == 0:
            fresh = fresh * inverse
        if last:
            out_ref[...] = fresh.astype(jnp.bfloat16)
        else:
            target_ref[...] = fresh.astype(jnp.bfloat16)
            source_ref, target_ref = target_ref, source_ref


def spread_kernel(table, table_any, returned_ref, total_ref, out_ref, table_ref, sem):
    copy = pltpu.make_async_copy(table_any, table_ref, sem)
    copy.start()
    per_group = total_ref.shape[0]
    for place in range(per_group):
        value = returned_ref[place]
        for target in range(out_ref.shape[0]):
            out_ref[target, place] = value
    value = total_ref[0]
    for target in range(out_ref.shape[0]):
        out_ref[target, per_group] = value
    copy.wait()
    for place in range(per_group):
        out_ref[table_ref[table.held_owner + place], per_group] = total_ref[place]


def update_kernel(
    table,
    scale,
    table_ref,
    both_ref,
    weight_ref,
    part_ref,
    momentum_ref,
    step_hbm,
    new_hbm,
    moved_hbm,
    step_ref,
    new_ref,
    moved_ref,
    sems,
    moved_sem,
):
    blocks, most = weight_ref.shape[0], momentum_ref.shape[0]
    each = blocks // PIECES
    leaving = []

    def leave(source, target, sem):
        leaving.append(pltpu.make_async_copy(source, target, sem))
        leaving[-1].start()

    for index in range(PIECES):
        chunk = pl.ds(index * each, each)
        for block in range(index * each, (index + 1) * each):
            step = both_ref[table_ref[table.block + block]].astype(jnp.float32) * scale
            step_ref[block] = step
            new_ref[block] = weight_ref[block] - LEARN_RATE * step
        leave(step_ref.at[chunk], step_hbm.at[chunk], sems.at[index, 0])
        leave(new_ref.at[chunk], new_hbm.at[chunk], sems.at[index, 1])
    count = table_ref[table.count]
    for slot in range(most):
        used = slot < count
        block = jnp.where(used, table_ref[table.own_block + slot], 0)
        source = jnp.where(used, table_ref[table.own_from + slot], 0) | (SEGMENT - 1)
        part = part_ref[block]
        before = momentum_ref[slot]
        added = folded(part, before).astype(jnp.float32) - part.astype(jnp.float32)
        gradient = both_ref[source].astype(jnp.float32) - added
        moved_ref[slot] = jnp.where(used, MOMENTUM_DECAY * before + gradient, before)
    leave(moved_ref, moved_hbm, moved_sem)
    for copy in leaving:
        copy.wait()


def call(kernel, out_shape, in_specs, scratch=(), flops=0, moved=0, out_specs=None, room=40.0):
    return pl.pallas_call(
        kernel,
        out_shape=out_shape,
        in_specs=in_specs,
        out_specs=jax.tree.map(lambda _: VMEM, out_shape) if out_specs is None else out_specs,
        scratch_shapes=list(scratch),
        compiler_params=pltpu.CompilerParams(vmem_limit_bytes=int((64 - room) * 1024 * 1024)),
        cost_estimate=pl.CostEstimate(flops=flops, bytes_accessed=moved, transcendentals=0),
    )


def on_device(grad_parts, momentum, weight, owners):
    part = grad_parts[0]
    blocks, rows, order = part.shape
    most = momentum.shape[0]
    groups = lax.axis_size("rep")
    members = lax.axis_size("fsdp")
    chips = members // 2
    per_group = blocks // groups
    table = Table(blocks, most, per_group)
    bf16 = functools.partial(jax.ShapeDtypeStruct, dtype=jnp.bfloat16)
    f32 = functools.partial(jax.ShapeDtypeStruct, dtype=jnp.float32)
    here = lax.axis_index("rep").astype(jnp.int32).reshape(1)
    segment = (lax.axis_index("fsdp") // (2 * SEGMENT)).astype(jnp.int32).reshape(1)
    same_core = [[2 * chip + core for chip in range(chips)] for core in range(2)]
    same_segment = [
        [2 * (SEGMENT * s + chip) + core for chip in range(SEGMENT)]
        for s in range(chips // SEGMENT)
        for core in range(2)
    ]

    with jax.named_scope("fold_momentum"):
        parts, places = call(
            functools.partial(fold_kernel, table, groups),
            [bf16((blocks, rows, order)), jax.ShapeDtypeStruct((table.size,), jnp.int32)],
            [SMEM, HBM, HBM, HBM],
            [
                pltpu.SMEM((table.size,), jnp.int32),
                pltpu.SMEM((blocks,), jnp.int32),
                pltpu.SMEM((groups,), jnp.int32),
                pltpu.SMEM((blocks,), jnp.int32),
                pltpu.VMEM(part.shape, jnp.bfloat16),
                pltpu.VMEM(momentum.shape, jnp.float32),
                pltpu.SemaphoreType.DMA((5,)),
            ],
            moved=1 << 21,
            out_specs=[HBM, HBM],
            room=1,
        )(here, owners, part, momentum)
    with jax.named_scope("reduce_over_rep"):
        received = lax.all_to_all(
            parts.reshape(groups, per_group, rows, order), "rep", 0, 0, tiled=True
        )
        send, total = call(
            sum_kernel,
            [bf16((chips, rows, order)), bf16((per_group, rows, order))],
            [VMEM],
            moved=1 << 20,
        )(received)
    with jax.named_scope("gather_rows"):
        own = lax.all_to_all(send, "fsdp", 0, 0, axis_index_groups=same_core, tiled=True)
        own = own.reshape(chips * rows, order)
        other = lax.ppermute(own, "fsdp", [(i, i ^ 1) for i in range(members)])
    with jax.named_scope("orthogonalize"):
        square = pltpu.VMEM((order, order), jnp.bfloat16)
        kept = call(
            newton_schulz_kernel,
            bf16((SEGMENT * rows, order)),
            [SMEM, VMEM, VMEM],
            [square] * 4,
            flops=15 * order**3,
            moved=1 << 20,
        )(segment, own, other)
    with jax.named_scope("return_rows"):
        returned = lax.all_to_all(
            kept.reshape(SEGMENT, rows, order), "fsdp", 0, 0, axis_index_groups=same_segment, tiled=True
        )
        spread = call(
            functools.partial(spread_kernel, table),
            bf16((groups, SEGMENT, rows, order)),
            [ANY, VMEM, VMEM],
            [pltpu.SMEM((table.size,), jnp.int32), pltpu.SemaphoreType.DMA],
            moved=1 << 20,
        )(places, returned, total)
        both = lax.all_to_all(spread, "rep", 0, 0, tiled=True).reshape(groups * SEGMENT, rows, order)
    with jax.named_scope("update"):
        return call(
            functools.partial(update_kernel, table, 0.2 * math.sqrt(order)),
            [f32(weight.shape), f32(weight.shape), f32(momentum.shape)],
            [SMEM, VMEM, VMEM, VMEM, VMEM],
            [
                pltpu.VMEM(weight.shape, jnp.float32),
                pltpu.VMEM(weight.shape, jnp.float32),
                pltpu.VMEM(momentum.shape, jnp.float32),
                pltpu.SemaphoreType.DMA((PIECES, 2)),
                pltpu.SemaphoreType.DMA,
            ],
            moved=5 << 20,
            out_specs=[HBM, HBM, HBM],
        )(places, both, weight, part, momentum)


def solution(mesh):
    return jax.shard_map(
        on_device,
        mesh=mesh,
        in_specs=(P("rep", None, "fsdp", None), P("rep", "fsdp", None), P(None, "fsdp", None), P()),
        out_specs=(P(None, "fsdp", None), P(None, "fsdp", None), P("rep", "fsdp", None)),
        check_vma=False,
    )
```

```python
import functools
import math

import jax
import jax.numpy as jnp
from jax import lax
from jax.experimental import pallas as pl
from jax.experimental.pallas import tpu as pltpu
from jax.sharding import PartitionSpec as P

NS_ITERS = 3
COEF_A = 3.4445
COEF_B = -4.775
COEF_C = 2.0315
MOMENTUM_DECAY = 0.95
LEARN_RATE = 0.02
EPSILON = 1e-07
DIRECTION_SCALE = 1.0 + MOMENTUM_DECAY
FOLD = MOMENTUM_DECAY * MOMENTUM_DECAY / DIRECTION_SCALE
SEGMENT = 4
PIECES = 6

VMEM = pl.BlockSpec(memory_space=pltpu.VMEM)
SMEM = pl.BlockSpec(memory_space=pltpu.SMEM)
HBM = pl.BlockSpec(memory_space=pltpu.HBM)
ANY = pl.BlockSpec(memory_space=pl.ANY)


def folded(part, momentum):
    return (part.astype(jnp.float32) + FOLD * momentum).astype(jnp.bfloat16)


def rank_blocks(groups, owners_ref, ranks_ref):
    blocks = owners_ref.shape[0]
    for group in range(groups):
        ranks_ref[blocks + group] = 0
    for block in range(blocks):
        owner = owners_ref[block]
        slot = ranks_ref[blocks + owner]
        ranks_ref[block] = slot
        ranks_ref[blocks + owner] = slot + 1
    first = jnp.int32(0)
    for group in range(groups):
        after = first + ranks_ref[blocks + group]
        ranks_ref[blocks + group] = first
        first = after
    for block in range(blocks):
        ranks_ref[block] = ranks_ref[blocks + owners_ref[block]] + ranks_ref[block]


def split_rank(groups, rank):
    return rank & (groups - 1), rank >> (groups.bit_length() - 1)


def list_owned(blocks, groups, here, ranks_ref, owned_ref):
    first = ranks_ref[blocks + here]
    after = jnp.where(here == groups - 1, blocks, ranks_ref[blocks + jnp.minimum(here + 1, groups - 1)])
    count = after - first
    unused = owned_ref.shape[0] - 1
    for block in range(blocks):
        slot = ranks_ref[block] - first
        owned_ref[jnp.where((slot >= 0) & (slot < count), slot, unused)] = block
    return first, count


def fold_kernel(
    groups,
    here_ref,
    owners_hbm,
    part_hbm,
    momentum_hbm,
    out_ref,
    ranks_out_ref,
    owners_ref,
    ranks_ref,
    owned_ref,
    part_ref,
    momentum_ref,
    sems,
):
    blocks, most = part_ref.shape[0], momentum_ref.shape[0]
    per_group = blocks // groups
    copies = [
        pltpu.make_async_copy(source, target, sems.at[index])
        for index, (source, target) in enumerate(
            [(owners_hbm, owners_ref), (part_hbm, part_ref), (momentum_hbm, momentum_ref)]
        )
    ]
    for copy in copies:
        copy.start()
    copies[0].wait()
    rank_blocks(groups, owners_ref, ranks_ref)
    ranks_out = pltpu.make_async_copy(ranks_ref, ranks_out_ref, sems.at[3])
    ranks_out.start()
    _, count = list_owned(blocks, groups, here_ref[0], ranks_ref, owned_ref)

    def target_of(block):
        group, place = split_rank(groups, ranks_ref[block])
        return group * per_group + place

    copies[1].wait()
    for block in range(blocks):
        out_ref[target_of(block)] = part_ref[block]
    copies[2].wait()
    for slot in range(most):

        @pl.when(slot < count)
        def _():
            block = owned_ref[slot]
            out_ref[target_of(block)] = folded(part_ref[block], momentum_ref[slot])

    ranks_out.wait()


def sum_kernel(parts_ref, send_ref, total_ref):
    count, blocks = parts_ref.shape[:2]
    for block in range(blocks):
        total = parts_ref[0, block].astype(jnp.float32)
        for source in range(1, count):
            total = total + parts_ref[source, block].astype(jnp.float32)
        total_ref[block] = total.astype(jnp.bfloat16)
        direction = (DIRECTION_SCALE * total).astype(jnp.bfloat16)
        for target in range(send_ref.shape[0]):
            if min(target % SEGMENT, blocks - 1) == block:
                send_ref[target] = direction


def dot_nt(a, b):
    return lax.dot_general(a, b, (((1,), (1,)), ((), ())), preferred_element_type=jnp.float32)


def dot_nn(a, b):
    return jnp.dot(a, b, preferred_element_type=jnp.float32)


def newton_schulz_kernel(segment_ref, own_ref, other_ref, out_ref, x_ref, y_ref, gram_ref, poly_ref):
    half, order = own_ref.shape
    kept = out_ref.shape[0]
    x_ref[0:half] = own_ref[...]
    x_ref[half:order] = other_ref[...]
    squares = jnp.zeros((8, order), jnp.float32)
    for ref in (own_ref, other_ref):
        wide = ref[...].astype(jnp.float32)
        squares = squares + jnp.sum((wide * wide).reshape(half // 8, 8, order), axis=0)
    inverse = 1.0 / (jnp.sqrt(jnp.sum(squares)) + EPSILON)
    source_ref, target_ref = x_ref, y_ref
    for iteration in range(NS_ITERS):
        gram = dot_nt(source_ref[...], source_ref[...])
        if iteration == 0:
            gram = gram * (inverse * inverse)
        gram_ref[...] = gram.astype(jnp.bfloat16)
        last = iteration == NS_ITERS - 1
        rows = pl.ds(pl.multiple_of(segment_ref[0] * kept, kept), kept) if last else pl.ds(0, order)
        gram = gram_ref[rows]
        poly = (COEF_B * gram.astype(jnp.float32) + COEF_C * dot_nn(gram, gram_ref[...])).astype(jnp.bfloat16)
        if not last:
            poly_ref[...] = poly
            poly = poly_ref[...]
        fresh = COEF_A * source_ref[rows].astype(jnp.float32) + dot_nn(poly, source_ref[...])
        if iteration == 0:
            fresh = fresh * inverse
        if last:
            out_ref[...] = fresh.astype(jnp.bfloat16)
        else:
            target_ref[...] = fresh.astype(jnp.bfloat16)
            source_ref, target_ref = target_ref, source_ref


def spread_kernel(groups, here_ref, ranks_any, returned_ref, total_ref, out_ref, ranks_ref, sem):
    copy = pltpu.make_async_copy(ranks_any, ranks_ref, sem)
    copy.start()
    per_group = total_ref.shape[0]
    blocks = groups * per_group
    for place in range(per_group):
        value = returned_ref[place]
        for target in range(groups):
            out_ref[target, place] = value
    value = total_ref[0]
    for target in range(groups):
        out_ref[target, per_group] = value
    copy.wait()
    for place in range(per_group):
        rank = place * groups + here_ref[0]
        owner = jnp.int32(-1)
        for group in range(groups):
            owner = owner + (ranks_ref[blocks + group] <= rank).astype(jnp.int32)
        out_ref[owner, per_group] = total_ref[place]


def update_kernel(
    groups,
    scale,
    here_ref,
    ranks_ref,
    both_ref,
    weight_ref,
    part_ref,
    momentum_ref,
    step_hbm,
    new_hbm,
    moved_hbm,
    owned_ref,
    step_ref,
    new_ref,
    moved_ref,
    sems,
    moved_sem,
):
    blocks, most = weight_ref.shape[0], momentum_ref.shape[0]
    per_group = blocks // groups
    each = blocks // PIECES
    leaving = []

    def leave(source, target, sem):
        leaving.append(pltpu.make_async_copy(source, target, sem))
        leaving[-1].start()

    for index in range(PIECES):
        chunk = pl.ds(index * each, each)
        for block in range(index * each, (index + 1) * each):
            group, place = split_rank(groups, ranks_ref[block])
            step = both_ref[group, place].astype(jnp.float32) * scale
            step_ref[block] = step
            new_ref[block] = weight_ref[block] - LEARN_RATE * step
        leave(step_ref.at[chunk], step_hbm.at[chunk], sems.at[index, 0])
        leave(new_ref.at[chunk], new_hbm.at[chunk], sems.at[index, 1])
    first, count = list_owned(blocks, groups, here_ref[0], ranks_ref, owned_ref)
    for slot in range(most):
        used = slot < count
        block = jnp.where(used, owned_ref[slot], 0)
        group, _ = split_rank(groups, first + slot)
        part = part_ref[block]
        before = momentum_ref[slot]
        added = folded(part, before).astype(jnp.float32) - part.astype(jnp.float32)
        gradient = both_ref[group, per_group].astype(jnp.float32) - added
        moved_ref[slot] = jnp.where(used, MOMENTUM_DECAY * before + gradient, before)
    leave(moved_ref, moved_hbm, moved_sem)
    for copy in leaving:
        copy.wait()


def call(kernel, out_shape, in_specs, scratch=(), flops=0, moved=0, out_specs=None, room=40.0):
    return pl.pallas_call(
        kernel,
        out_shape=out_shape,
        in_specs=in_specs,
        out_specs=jax.tree.map(lambda _: VMEM, out_shape) if out_specs is None else out_specs,
        scratch_shapes=list(scratch),
        compiler_params=pltpu.CompilerParams(vmem_limit_bytes=int((64 - room) * 1024 * 1024)),
        cost_estimate=pl.CostEstimate(flops=flops, bytes_accessed=moved, transcendentals=0),
    )


def on_device(grad_parts, momentum, weight, owners):
    part = grad_parts[0]
    blocks, rows, order = part.shape
    most = momentum.shape[0]
    groups = lax.axis_size("rep")
    members = lax.axis_size("fsdp")
    chips = members // 2
    per_group = blocks // groups
    ranks_size = blocks + groups
    bf16 = functools.partial(jax.ShapeDtypeStruct, dtype=jnp.bfloat16)
    f32 = functools.partial(jax.ShapeDtypeStruct, dtype=jnp.float32)
    here = lax.axis_index("rep").astype(jnp.int32).reshape(1)
    segment = (lax.axis_index("fsdp") // (2 * SEGMENT)).astype(jnp.int32).reshape(1)
    same_core = [[2 * chip + core for chip in range(chips)] for core in range(2)]
    same_segment = [
        [2 * (SEGMENT * s + chip) + core for chip in range(SEGMENT)]
        for s in range(chips // SEGMENT)
        for core in range(2)
    ]

    with jax.named_scope("fold_momentum"):
        parts, ranks = call(
            functools.partial(fold_kernel, groups),
            [pltpu.VMEM((blocks, rows, order), jnp.bfloat16), pltpu.VMEM((ranks_size,), jnp.int32)],
            [SMEM, HBM, HBM, HBM],
            [
                pltpu.SMEM((blocks,), jnp.int32),
                pltpu.SMEM((ranks_size,), jnp.int32),
                pltpu.SMEM((most + 1,), jnp.int32),
                pltpu.VMEM(part.shape, jnp.bfloat16),
                pltpu.VMEM(momentum.shape, jnp.float32),
                pltpu.SemaphoreType.DMA((4,)),
            ],
            moved=1 << 21,
        )(here, *(pltpu.with_memory_space_constraint(array, pltpu.HBM) for array in (owners, part, momentum)))
    with jax.named_scope("reduce_over_rep"):
        received = lax.all_to_all(
            parts.reshape(groups, per_group, rows, order), "rep", 0, 0, tiled=True
        )
        send, total = call(
            sum_kernel,
            [bf16((chips, rows, order)), bf16((per_group, rows, order))],
            [VMEM],
            moved=1 << 20,
        )(received)
    with jax.named_scope("gather_rows"):
        own = lax.all_to_all(send, "fsdp", 0, 0, axis_index_groups=same_core, tiled=True)
        own = own.reshape(chips * rows, order)
        other = lax.ppermute(own, "fsdp", [(i, i ^ 1) for i in range(members)])
    with jax.named_scope("orthogonalize"):
        square = pltpu.VMEM((order, order), jnp.bfloat16)
        kept = call(
            newton_schulz_kernel,
            bf16((SEGMENT * rows, order)),
            [SMEM, VMEM, VMEM],
            [square] * 4,
            flops=15 * order**3,
            moved=1 << 20,
        )(segment, own, other)
    with jax.named_scope("return_rows"):
        returned = lax.all_to_all(
            kept.reshape(SEGMENT, rows, order), "fsdp", 0, 0, axis_index_groups=same_segment, tiled=True
        )
        spread = call(
            functools.partial(spread_kernel, groups),
            bf16((groups, per_group + 1, rows, order)),
            [SMEM, ANY, VMEM, VMEM],
            [pltpu.SMEM((ranks_size,), jnp.int32), pltpu.SemaphoreType.DMA],
            moved=1 << 20,
        )(here, ranks, returned, total)
        both = lax.all_to_all(spread, "rep", 0, 0, tiled=True)
    with jax.named_scope("update"):
        return call(
            functools.partial(update_kernel, groups, 0.2 * math.sqrt(order)),
            [f32(weight.shape), f32(weight.shape), f32(momentum.shape)],
            [SMEM, SMEM, VMEM, VMEM, VMEM, VMEM],
            [
                pltpu.SMEM((most + 1,), jnp.int32),
                pltpu.VMEM(weight.shape, jnp.float32),
                pltpu.VMEM(weight.shape, jnp.float32),
                pltpu.VMEM(momentum.shape, jnp.float32),
                pltpu.SemaphoreType.DMA((PIECES, 2)),
                pltpu.SemaphoreType.DMA,
            ],
            moved=5 << 20,
            out_specs=[HBM, HBM, HBM],
        )(here, ranks, both, weight, part, momentum)


def solution(mesh):
    return jax.shard_map(
        on_device,
        mesh=mesh,
        in_specs=(P("rep", None, "fsdp", None), P("rep", "fsdp", None), P(None, "fsdp", None), P()),
        out_specs=(P(None, "fsdp", None), P(None, "fsdp", None), P("rep", "fsdp", None)),
        check_vma=False,
    )
```

```python
import functools
import math

import jax
import jax.numpy as jnp
from jax import lax
from jax.experimental import pallas as pl
from jax.experimental.pallas import tpu as pltpu
from jax.sharding import PartitionSpec as P

NS_ITERS = 3
COEF_A = 3.4445
COEF_B = -4.775
COEF_C = 2.0315
MOMENTUM_DECAY = 0.95
LEARN_RATE = 0.02
EPSILON = 1e-07
DIRECTION_SCALE = 1.0 + MOMENTUM_DECAY
FOLD = MOMENTUM_DECAY * MOMENTUM_DECAY / DIRECTION_SCALE
SEGMENT = 4
PIECES = 6
FIRST_GROUP = 14
TOP_SEGMENTS = 3
SEGMENT_ORDER = (2, 1, 3, 0)

VMEM = pl.BlockSpec(memory_space=pltpu.VMEM)
SMEM = pl.BlockSpec(memory_space=pltpu.SMEM)
HBM = pl.BlockSpec(memory_space=pltpu.HBM)
ANY = pl.BlockSpec(memory_space=pl.ANY)


def folded(part, momentum):
    return (part.astype(jnp.float32) + FOLD * momentum).astype(jnp.bfloat16)


def rank_blocks(groups, owners_ref, ranks_ref):
    blocks = owners_ref.shape[0]
    for group in range(groups):
        ranks_ref[blocks + group] = 0
    for block in range(blocks):
        owner = owners_ref[block]
        slot = ranks_ref[blocks + owner]
        ranks_ref[block] = slot
        ranks_ref[blocks + owner] = slot + 1
    first = jnp.int32(0)
    for group in range(groups):
        after = first + ranks_ref[blocks + group]
        ranks_ref[blocks + group] = first
        first = after
    for block in range(blocks):
        ranks_ref[block] = ranks_ref[blocks + owners_ref[block]] + ranks_ref[block]


def split_rank(groups, rank):
    return rank & (groups - 1), rank >> (groups.bit_length() - 1)


def list_owned(blocks, groups, here, ranks_ref, owned_ref):
    first = ranks_ref[blocks + here]
    after = jnp.where(here == groups - 1, blocks, ranks_ref[blocks + jnp.minimum(here + 1, groups - 1)])
    count = after - first
    unused = owned_ref.shape[0] - 1
    for block in range(blocks):
        slot = ranks_ref[block] - first
        owned_ref[jnp.where((slot >= 0) & (slot < count), slot, unused)] = block
    return first, count


def fold_kernel(
    groups,
    here_ref,
    owners_hbm,
    part_hbm,
    momentum_hbm,
    out_ref,
    ranks_out_ref,
    owners_ref,
    ranks_ref,
    owned_ref,
    part_ref,
    momentum_ref,
    sems,
):
    blocks, most = part_ref.shape[0], momentum_ref.shape[0]
    per_group = blocks // groups
    copies = [
        pltpu.make_async_copy(source, target, sems.at[index])
        for index, (source, target) in enumerate(
            [(owners_hbm, owners_ref), (part_hbm, part_ref), (momentum_hbm, momentum_ref)]
        )
    ]
    for copy in copies:
        copy.start()
    copies[0].wait()
    rank_blocks(groups, owners_ref, ranks_ref)
    ranks_out = pltpu.make_async_copy(ranks_ref, ranks_out_ref, sems.at[3])
    ranks_out.start()
    _, count = list_owned(blocks, groups, here_ref[0], ranks_ref, owned_ref)

    def target_of(block):
        group, place = split_rank(groups, ranks_ref[block])
        return ((group - FIRST_GROUP) & (groups - 1)) * per_group + place

    copies[1].wait()
    for block in range(blocks):
        out_ref[target_of(block)] = part_ref[block]
    copies[2].wait()
    for slot in range(most):

        @pl.when(slot < count)
        def _():
            block = owned_ref[slot]
            out_ref[target_of(block)] = folded(part_ref[block], momentum_ref[slot])

    ranks_out.wait()


def sum_kernel(ring, parts_ref, send_ref, total_ref):
    count, blocks = parts_ref.shape[:2]
    for block in range(blocks):
        total = parts_ref[0, block].astype(jnp.float32)
        for source in range(1, count):
            total = total + parts_ref[source, block].astype(jnp.float32)
        total_ref[block] = total.astype(jnp.bfloat16)
        direction = (DIRECTION_SCALE * total).astype(jnp.bfloat16)
        for target, chip in enumerate(ring):
            if min(chip % SEGMENT, blocks - 1) == block:
                send_ref[target] = direction


def dot_nt(a, b):
    return lax.dot_general(a, b, (((1,), (1,)), ((), ())), preferred_element_type=jnp.float32)


def dot_nn(a, b):
    return jnp.dot(a, b, preferred_element_type=jnp.float32)


def newton_schulz_kernel(first_ref, own_ref, other_ref, out_ref, x_ref, y_ref, gram_ref, poly_ref):
    half, order = own_ref.shape
    kept = out_ref.shape[0]
    x_ref[0:half] = own_ref[...]
    x_ref[half:order] = other_ref[...]
    squares = jnp.zeros((8, order), jnp.float32)
    for ref in (own_ref, other_ref):
        wide = ref[...].astype(jnp.float32)
        squares = squares + jnp.sum((wide * wide).reshape(half // 8, 8, order), axis=0)
    inverse = 1.0 / (jnp.sqrt(jnp.sum(squares)) + EPSILON)
    source_ref, target_ref = x_ref, y_ref
    for iteration in range(NS_ITERS):
        gram = dot_nt(source_ref[...], source_ref[...])
        if iteration == 0:
            gram = gram * (inverse * inverse)
        gram_ref[...] = gram.astype(jnp.bfloat16)
        last = iteration == NS_ITERS - 1
        rows = pl.ds(pl.multiple_of(first_ref[0] * kept, kept), kept) if last else pl.ds(0, order)
        gram = gram_ref[rows]
        poly = (COEF_B * gram.astype(jnp.float32) + COEF_C * dot_nn(gram, gram_ref[...])).astype(jnp.bfloat16)
        if not last:
            poly_ref[...] = poly
            poly = poly_ref[...]
        fresh = COEF_A * source_ref[rows].astype(jnp.float32) + dot_nn(poly, source_ref[...])
        if iteration == 0:
            fresh = fresh * inverse
        if last:
            each = kept // SEGMENT
            for target, chip in enumerate(SEGMENT_ORDER):
                start = (SEGMENT - 1 - chip) * each
                out_ref[target * each : (target + 1) * each] = fresh[start : start + each].astype(jnp.bfloat16)
        else:
            target_ref[...] = fresh.astype(jnp.bfloat16)
            source_ref, target_ref = target_ref, source_ref


def spread_kernel(groups, here_ref, ranks_any, returned_ref, total_ref, out_ref, ranks_ref, sem):
    copy = pltpu.make_async_copy(ranks_any, ranks_ref, sem)
    copy.start()
    per_group = total_ref.shape[0]
    blocks = groups * per_group
    for place in range(per_group):
        value = returned_ref[SEGMENT_ORDER.index(place)]
        for target in range(groups):
            out_ref[target, place] = value
    value = total_ref[0]
    for target in range(groups):
        out_ref[target, per_group] = value
    copy.wait()
    for place in range(per_group):
        rank = place * groups + here_ref[0]
        owner = jnp.int32(-1)
        for group in range(groups):
            owner = owner + (ranks_ref[blocks + group] <= rank).astype(jnp.int32)
        out_ref[owner, per_group] = total_ref[place]


def update_kernel(
    groups,
    scale,
    here_ref,
    ranks_ref,
    both_ref,
    weight_ref,
    part_ref,
    momentum_ref,
    step_hbm,
    new_hbm,
    moved_hbm,
    owned_ref,
    step_ref,
    new_ref,
    moved_ref,
    sems,
    moved_sem,
):
    blocks, most = weight_ref.shape[0], momentum_ref.shape[0]
    per_group = blocks // groups
    each = blocks // PIECES
    leaving = []

    def leave(source, target, sem):
        leaving.append(pltpu.make_async_copy(source, target, sem))
        leaving[-1].start()

    for index in range(PIECES):
        chunk = pl.ds(index * each, each)
        for block in range(index * each, (index + 1) * each):
            group, place = split_rank(groups, ranks_ref[block])
            step = both_ref[group, place].astype(jnp.float32) * scale
            step_ref[block] = step
            new_ref[block] = weight_ref[block] - LEARN_RATE * step
        leave(step_ref.at[chunk], step_hbm.at[chunk], sems.at[index, 0])
        leave(new_ref.at[chunk], new_hbm.at[chunk], sems.at[index, 1])
    first, count = list_owned(blocks, groups, here_ref[0], ranks_ref, owned_ref)
    for slot in range(most):
        used = slot < count
        block = jnp.where(used, owned_ref[slot], 0)
        group, _ = split_rank(groups, first + slot)
        part = part_ref[block]
        before = momentum_ref[slot]
        added = folded(part, before).astype(jnp.float32) - part.astype(jnp.float32)
        gradient = both_ref[group, per_group].astype(jnp.float32) - added
        moved_ref[slot] = jnp.where(used, MOMENTUM_DECAY * before + gradient, before)
    leave(moved_ref, moved_hbm, moved_sem)
    for copy in leaving:
        copy.wait()


def call(kernel, out_shape, in_specs, scratch=(), flops=0, moved=0, out_specs=None, room=40.0):
    return pl.pallas_call(
        kernel,
        out_shape=out_shape,
        in_specs=in_specs,
        out_specs=jax.tree.map(lambda _: VMEM, out_shape) if out_specs is None else out_specs,
        scratch_shapes=list(scratch),
        compiler_params=pltpu.CompilerParams(vmem_limit_bytes=int((64 - room) * 1024 * 1024)),
        cost_estimate=pl.CostEstimate(flops=flops, bytes_accessed=moved, transcendentals=0),
    )


def on_device(grad_parts, momentum, weight, owners):
    part = grad_parts[0]
    blocks, rows, order = part.shape
    most = momentum.shape[0]
    groups = lax.axis_size("rep")
    members = lax.axis_size("fsdp")
    chips = members // 2
    per_group = blocks // groups
    ranks_size = blocks + groups
    bf16 = functools.partial(jax.ShapeDtypeStruct, dtype=jnp.bfloat16)
    f32 = functools.partial(jax.ShapeDtypeStruct, dtype=jnp.float32)
    here = lax.axis_index("rep").astype(jnp.int32).reshape(1)
    segments = chips // SEGMENT
    ring = [(SEGMENT * TOP_SEGMENTS - 1 - index) % chips for index in range(chips)]
    same_core = [[2 * chip + core for chip in ring] for core in range(2)]
    same_segment = [
        [2 * (SEGMENT * s + chip) + core for chip in SEGMENT_ORDER] for s in range(segments) for core in range(2)
    ]
    from_first = [[(FIRST_GROUP + index) % groups for index in range(groups)]]
    segment = lax.axis_index("fsdp") // (2 * SEGMENT)
    listed = lax.rem(TOP_SEGMENTS - 1 + segments - segment, segments).astype(jnp.int32).reshape(1)

    with jax.named_scope("fold_momentum"):
        parts, ranks = call(
            functools.partial(fold_kernel, groups),
            [pltpu.VMEM((blocks, rows, order), jnp.bfloat16), pltpu.VMEM((ranks_size,), jnp.int32)],
            [SMEM, HBM, HBM, HBM],
            [
                pltpu.SMEM((blocks,), jnp.int32),
                pltpu.SMEM((ranks_size,), jnp.int32),
                pltpu.SMEM((most + 1,), jnp.int32),
                pltpu.VMEM(part.shape, jnp.bfloat16),
                pltpu.VMEM(momentum.shape, jnp.float32),
                pltpu.SemaphoreType.DMA((4,)),
            ],
            moved=1 << 21,
        )(here, *(pltpu.with_memory_space_constraint(array, pltpu.HBM) for array in (owners, part, momentum)))
    with jax.named_scope("reduce_over_rep"):
        received = lax.all_to_all(
            parts.reshape(groups, per_group, rows, order),
            "rep",
            0,
            0,
            axis_index_groups=from_first,
            tiled=True,
        )
        send, total = call(
            functools.partial(sum_kernel, ring),
            [bf16((chips, rows, order)), bf16((per_group, rows, order))],
            [VMEM],
            moved=1 << 20,
        )(received)
    with jax.named_scope("gather_rows"):
        own = lax.all_to_all(send, "fsdp", 0, 0, axis_index_groups=same_core, tiled=True)
        own = own.reshape(chips * rows, order)
        other = lax.ppermute(own, "fsdp", [(i, i ^ 1) for i in range(members)])
    with jax.named_scope("orthogonalize"):
        square = pltpu.VMEM((order, order), jnp.bfloat16)
        kept = call(
            newton_schulz_kernel,
            bf16((SEGMENT * rows, order)),
            [SMEM, VMEM, VMEM],
            [square] * 4,
            flops=15 * order**3,
            moved=1 << 20,
        )(listed, own, other)
    with jax.named_scope("return_rows"):
        returned = lax.all_to_all(
            kept.reshape(SEGMENT, rows, order), "fsdp", 0, 0, axis_index_groups=same_segment, tiled=True
        )
        spread = call(
            functools.partial(spread_kernel, groups),
            bf16((groups, per_group + 1, rows, order)),
            [SMEM, ANY, VMEM, VMEM],
            [pltpu.SMEM((ranks_size,), jnp.int32), pltpu.SemaphoreType.DMA],
            moved=1 << 20,
        )(here, ranks, returned, total)
        both = lax.all_to_all(spread, "rep", 0, 0, tiled=True)
    with jax.named_scope("update"):
        return call(
            functools.partial(update_kernel, groups, 0.2 * math.sqrt(order)),
            [f32(weight.shape), f32(weight.shape), f32(momentum.shape)],
            [SMEM, SMEM, VMEM, VMEM, VMEM, VMEM],
            [
                pltpu.SMEM((most + 1,), jnp.int32),
                pltpu.VMEM(weight.shape, jnp.float32),
                pltpu.VMEM(weight.shape, jnp.float32),
                pltpu.VMEM(momentum.shape, jnp.float32),
                pltpu.SemaphoreType.DMA((PIECES, 2)),
                pltpu.SemaphoreType.DMA,
            ],
            moved=5 << 20,
            out_specs=[HBM, HBM, HBM],
        )(here, ranks, both, weight, part, momentum)


def solution(mesh):
    return jax.shard_map(
        on_device,
        mesh=mesh,
        in_specs=(P("rep", None, "fsdp", None), P("rep", "fsdp", None), P(None, "fsdp", None), P()),
        out_specs=(P(None, "fsdp", None), P(None, "fsdp", None), P("rep", "fsdp", None)),
        check_vma=False,
    )
```

```python
import functools
import math

import jax
import jax.numpy as jnp
from jax import lax
from jax.experimental import pallas as pl
from jax.experimental.pallas import tpu as pltpu
from jax.sharding import PartitionSpec as P

NS_ITERS = 3
COEF_A = 3.4445
COEF_B = -4.775
COEF_C = 2.0315
MOMENTUM_DECAY = 0.95
LEARN_RATE = 0.02
EPSILON = 1e-07
DIRECTION_SCALE = 1.0 + MOMENTUM_DECAY
FOLD = MOMENTUM_DECAY * MOMENTUM_DECAY / DIRECTION_SCALE
SEGMENT = 4
PIECES = 6
FIRST_GROUP = 14
TOP_SEGMENTS = 3
SEGMENT_ORDER = (2, 1, 3, 0)

VMEM = pl.BlockSpec(memory_space=pltpu.VMEM)
SMEM = pl.BlockSpec(memory_space=pltpu.SMEM)
HBM = pl.BlockSpec(memory_space=pltpu.HBM)


def folded(part, momentum):
    return (part.astype(jnp.float32) + FOLD * momentum).astype(jnp.bfloat16)


def rank_blocks(groups, owners_ref, ranks_ref):
    blocks = owners_ref.shape[0]
    for group in range(groups):
        ranks_ref[blocks + group] = 0
    for block in range(blocks):
        owner = owners_ref[block]
        slot = ranks_ref[blocks + owner]
        ranks_ref[block] = slot
        ranks_ref[blocks + owner] = slot + 1
    first = jnp.int32(0)
    for group in range(groups):
        after = first + ranks_ref[blocks + group]
        ranks_ref[blocks + group] = first
        first = after
    for block in range(blocks):
        ranks_ref[block] = ranks_ref[blocks + owners_ref[block]] + ranks_ref[block]


def split_rank(groups, rank):
    return rank & (groups - 1), rank >> (groups.bit_length() - 1)


def list_owned(blocks, groups, here, ranks_ref, owned_ref):
    first = ranks_ref[blocks + here]
    after = jnp.where(here == groups - 1, blocks, ranks_ref[blocks + jnp.minimum(here + 1, groups - 1)])
    count = after - first
    unused = owned_ref.shape[0] - 1
    for block in range(blocks):
        slot = ranks_ref[block] - first
        owned_ref[jnp.where((slot >= 0) & (slot < count), slot, unused)] = block
    return first, count


def fold_kernel(
    groups,
    here_ref,
    owners_hbm,
    part_hbm,
    momentum_hbm,
    out_ref,
    owners_ref,
    ranks_ref,
    owned_ref,
    part_ref,
    momentum_ref,
    sems,
):
    blocks, most = part_ref.shape[0], momentum_ref.shape[0]
    per_group = blocks // groups
    copies = [
        pltpu.make_async_copy(source, target, sems.at[index])
        for index, (source, target) in enumerate(
            [(owners_hbm, owners_ref), (part_hbm, part_ref), (momentum_hbm, momentum_ref)]
        )
    ]
    for copy in copies:
        copy.start()
    copies[0].wait()
    rank_blocks(groups, owners_ref, ranks_ref)
    _, count = list_owned(blocks, groups, here_ref[0], ranks_ref, owned_ref)

    def target_of(block):
        group, place = split_rank(groups, ranks_ref[block])
        return ((group - FIRST_GROUP) & (groups - 1)) * per_group + place

    copies[1].wait()
    for block in range(blocks):
        out_ref[target_of(block)] = part_ref[block]
    copies[2].wait()
    for slot in range(most):

        @pl.when(slot < count)
        def _():
            block = owned_ref[slot]
            out_ref[target_of(block)] = folded(part_ref[block], momentum_ref[slot])


def sums_kernel(groups, here_ref, owners_ref, total_ref, out_ref, ranks_out_ref, ranks_ref, sem):
    rank_blocks(groups, owners_ref, ranks_ref)
    copy = pltpu.make_async_copy(ranks_ref, ranks_out_ref, sem)
    copy.start()
    per_group = total_ref.shape[0]
    blocks = groups * per_group
    value = total_ref[0]
    for target in range(groups):
        out_ref[target, per_group] = value
    for place in range(per_group):
        rank = place * groups + here_ref[0]
        owner = jnp.int32(-1)
        for group in range(groups):
            owner = owner + (ranks_ref[blocks + group] <= rank).astype(jnp.int32)
        out_ref[owner, per_group] = total_ref[place]
    copy.wait()


def sum_kernel(ring, parts_ref, send_ref, total_ref):
    count, blocks = parts_ref.shape[:2]
    for block in range(blocks):
        total = parts_ref[0, block].astype(jnp.float32)
        for source in range(1, count):
            total = total + parts_ref[source, block].astype(jnp.float32)
        total_ref[block] = total.astype(jnp.bfloat16)
        direction = (DIRECTION_SCALE * total).astype(jnp.bfloat16)
        for target, chip in enumerate(ring):
            if min(chip % SEGMENT, blocks - 1) == block:
                send_ref[target] = direction


def dot_nt(a, b):
    return lax.dot_general(a, b, (((1,), (1,)), ((), ())), preferred_element_type=jnp.float32)


def dot_nn(a, b):
    return jnp.dot(a, b, preferred_element_type=jnp.float32)


def newton_schulz_kernel(first_ref, own_ref, other_ref, out_ref, x_ref, y_ref, gram_ref, poly_ref):
    half, order = own_ref.shape
    kept = out_ref.shape[0]
    x_ref[0:half] = own_ref[...]
    x_ref[half:order] = other_ref[...]
    squares = jnp.zeros((8, order), jnp.float32)
    for ref in (own_ref, other_ref):
        wide = ref[...].astype(jnp.float32)
        squares = squares + jnp.sum((wide * wide).reshape(half // 8, 8, order), axis=0)
    inverse = 1.0 / (jnp.sqrt(jnp.sum(squares)) + EPSILON)
    source_ref, target_ref = x_ref, y_ref
    for iteration in range(NS_ITERS):
        gram = dot_nt(source_ref[...], source_ref[...])
        if iteration == 0:
            gram = gram * (inverse * inverse)
        gram_ref[...] = gram.astype(jnp.bfloat16)
        last = iteration == NS_ITERS - 1
        rows = pl.ds(pl.multiple_of(first_ref[0] * kept, kept), kept) if last else pl.ds(0, order)
        gram = gram_ref[rows]
        poly = (COEF_B * gram.astype(jnp.float32) + COEF_C * dot_nn(gram, gram_ref[...])).astype(jnp.bfloat16)
        if not last:
            poly_ref[...] = poly
            poly = poly_ref[...]
        fresh = COEF_A * source_ref[rows].astype(jnp.float32) + dot_nn(poly, source_ref[...])
        if iteration == 0:
            fresh = fresh * inverse
        if last:
            each = kept // SEGMENT
            for target, chip in enumerate(SEGMENT_ORDER):
                start = (SEGMENT - 1 - chip) * each
                out_ref[target * each : (target + 1) * each] = fresh[start : start + each].astype(jnp.bfloat16)
        else:
            target_ref[...] = fresh.astype(jnp.bfloat16)
            source_ref, target_ref = target_ref, source_ref


def spread_kernel(returned_ref, sums_ref, out_ref):
    del sums_ref
    for place in range(out_ref.shape[1] - 1):
        value = returned_ref[SEGMENT_ORDER.index(place)]
        for target in range(out_ref.shape[0]):
            out_ref[target, place] = value


def update_kernel(
    groups,
    scale,
    here_ref,
    ranks_ref,
    both_ref,
    weight_ref,
    part_ref,
    momentum_ref,
    step_hbm,
    new_hbm,
    moved_hbm,
    owned_ref,
    step_ref,
    new_ref,
    moved_ref,
    sems,
    moved_sem,
):
    blocks, most = weight_ref.shape[0], momentum_ref.shape[0]
    per_group = blocks // groups
    each = blocks // PIECES
    leaving = []

    def leave(source, target, sem):
        leaving.append(pltpu.make_async_copy(source, target, sem))
        leaving[-1].start()

    for index in range(PIECES):
        chunk = pl.ds(index * each, each)
        for block in range(index * each, (index + 1) * each):
            group, place = split_rank(groups, ranks_ref[block])
            step = both_ref[group, place].astype(jnp.float32) * scale
            step_ref[block] = step
            new_ref[block] = weight_ref[block] - LEARN_RATE * step
        leave(step_ref.at[chunk], step_hbm.at[chunk], sems.at[index, 0])
        leave(new_ref.at[chunk], new_hbm.at[chunk], sems.at[index, 1])
    first, count = list_owned(blocks, groups, here_ref[0], ranks_ref, owned_ref)
    for slot in range(most):
        used = slot < count
        block = jnp.where(used, owned_ref[slot], 0)
        group, _ = split_rank(groups, first + slot)
        part = part_ref[block]
        before = momentum_ref[slot]
        added = folded(part, before).astype(jnp.float32) - part.astype(jnp.float32)
        gradient = both_ref[group, per_group].astype(jnp.float32) - added
        moved_ref[slot] = jnp.where(used, MOMENTUM_DECAY * before + gradient, before)
    leave(moved_ref, moved_hbm, moved_sem)
    for copy in leaving:
        copy.wait()


def call(kernel, out_shape, in_specs, scratch=(), flops=0, moved=0, out_specs=None, room=40.0, aliases={}):
    return pl.pallas_call(
        kernel,
        out_shape=out_shape,
        in_specs=in_specs,
        out_specs=jax.tree.map(lambda _: VMEM, out_shape) if out_specs is None else out_specs,
        scratch_shapes=list(scratch),
        input_output_aliases=aliases,
        compiler_params=pltpu.CompilerParams(vmem_limit_bytes=int((64 - room) * 1024 * 1024)),
        cost_estimate=pl.CostEstimate(flops=flops, bytes_accessed=moved, transcendentals=0),
    )


def on_device(grad_parts, momentum, weight, owners):
    part = grad_parts[0]
    blocks, rows, order = part.shape
    most = momentum.shape[0]
    groups = lax.axis_size("rep")
    members = lax.axis_size("fsdp")
    chips = members // 2
    per_group = blocks // groups
    ranks_size = blocks + groups
    bf16 = functools.partial(jax.ShapeDtypeStruct, dtype=jnp.bfloat16)
    f32 = functools.partial(jax.ShapeDtypeStruct, dtype=jnp.float32)
    here = lax.axis_index("rep").astype(jnp.int32).reshape(1)
    segments = chips // SEGMENT
    ring = [(SEGMENT * TOP_SEGMENTS - 1 - index) % chips for index in range(chips)]
    same_core = [[2 * chip + core for chip in ring] for core in range(2)]
    same_segment = [
        [2 * (SEGMENT * s + chip) + core for chip in SEGMENT_ORDER] for s in range(segments) for core in range(2)
    ]
    from_first = [[(FIRST_GROUP + index) % groups for index in range(groups)]]
    segment = lax.axis_index("fsdp") // (2 * SEGMENT)
    listed = lax.rem(TOP_SEGMENTS - 1 + segments - segment, segments).astype(jnp.int32).reshape(1)

    with jax.named_scope("fold_momentum"):
        parts = call(
            functools.partial(fold_kernel, groups),
            pltpu.VMEM((blocks, rows, order), jnp.bfloat16),
            [SMEM, HBM, HBM, HBM],
            [
                pltpu.SMEM((blocks,), jnp.int32),
                pltpu.SMEM((ranks_size,), jnp.int32),
                pltpu.SMEM((most + 1,), jnp.int32),
                pltpu.VMEM(part.shape, jnp.bfloat16),
                pltpu.VMEM(momentum.shape, jnp.float32),
                pltpu.SemaphoreType.DMA((3,)),
            ],
            moved=1 << 21,
        )(here, *(pltpu.with_memory_space_constraint(array, pltpu.HBM) for array in (owners, part, momentum)))
    with jax.named_scope("reduce_over_rep"):
        received = lax.all_to_all(
            parts.reshape(groups, per_group, rows, order),
            "rep",
            0,
            0,
            axis_index_groups=from_first,
            tiled=True,
        )
        send, total = call(
            functools.partial(sum_kernel, ring),
            [bf16((chips, rows, order)), bf16((per_group, rows, order))],
            [VMEM],
            moved=1 << 20,
        )(received)
    with jax.named_scope("gather_rows"):
        own = lax.all_to_all(send, "fsdp", 0, 0, axis_index_groups=same_core, tiled=True)
        own = own.reshape(chips * rows, order)
        other = lax.ppermute(own, "fsdp", [(i, i ^ 1) for i in range(members)])
    with jax.named_scope("sums_to_owners"):
        late_owners, own = lax.optimization_barrier((owners, own))
        sums, ranks = call(
            functools.partial(sums_kernel, groups),
            [
                pltpu.VMEM((groups, per_group + 1, rows, order), jnp.bfloat16),
                pltpu.VMEM((ranks_size,), jnp.int32),
            ],
            [SMEM, SMEM, VMEM],
            [pltpu.SMEM((ranks_size,), jnp.int32), pltpu.SemaphoreType.DMA],
            moved=1 << 20,
        )(here, late_owners, total)
        other, ranks = lax.optimization_barrier((other, ranks))
    with jax.named_scope("orthogonalize"):
        square = pltpu.VMEM((order, order), jnp.bfloat16)
        kept = call(
            newton_schulz_kernel,
            bf16((SEGMENT * rows, order)),
            [SMEM, VMEM, VMEM],
            [square] * 4,
            flops=15 * order**3,
            moved=1 << 20,
        )(listed, own, other)
    with jax.named_scope("return_rows"):
        returned = lax.all_to_all(
            kept.reshape(SEGMENT, rows, order), "fsdp", 0, 0, axis_index_groups=same_segment, tiled=True
        )
        spread = call(
            spread_kernel,
            bf16(sums.shape),
            [VMEM, VMEM],
            moved=1 << 20,
            aliases={1: 0},
        )(returned, sums)
        both = lax.all_to_all(spread, "rep", 0, 0, tiled=True)
    with jax.named_scope("update"):
        return call(
            functools.partial(update_kernel, groups, 0.2 * math.sqrt(order)),
            [f32(weight.shape), f32(weight.shape), f32(momentum.shape)],
            [SMEM, SMEM, VMEM, VMEM, VMEM, VMEM],
            [
                pltpu.SMEM((most + 1,), jnp.int32),
                pltpu.VMEM(weight.shape, jnp.float32),
                pltpu.VMEM(weight.shape, jnp.float32),
                pltpu.VMEM(momentum.shape, jnp.float32),
                pltpu.SemaphoreType.DMA((PIECES, 2)),
                pltpu.SemaphoreType.DMA,
            ],
            moved=5 << 20,
            out_specs=[HBM, HBM, HBM],
        )(here, ranks, both, weight, part, momentum)


def solution(mesh):
    return jax.shard_map(
        on_device,
        mesh=mesh,
        in_specs=(P("rep", None, "fsdp", None), P("rep", "fsdp", None), P(None, "fsdp", None), P()),
        out_specs=(P(None, "fsdp", None), P(None, "fsdp", None), P("rep", "fsdp", None)),
        check_vma=False,
    )
```

```python
import functools
import math

import jax
import jax.numpy as jnp
from jax import lax
from jax.experimental import pallas as pl
from jax.experimental.pallas import tpu as pltpu
from jax.sharding import PartitionSpec as P

NS_ITERS = 3
COEF_A = 3.4445
COEF_B = -4.775
COEF_C = 2.0315
MOMENTUM_DECAY = 0.95
LEARN_RATE = 0.02
EPSILON = 1e-07
DIRECTION_SCALE = 1.0 + MOMENTUM_DECAY
FOLD = MOMENTUM_DECAY * MOMENTUM_DECAY / DIRECTION_SCALE
SEGMENT = 4
PIECES = 6
FIRST_GROUP = 14
TOP_SEGMENTS = 3
SEGMENT_ORDER = (2, 1, 3, 0)

VMEM = pl.BlockSpec(memory_space=pltpu.VMEM)
SMEM = pl.BlockSpec(memory_space=pltpu.SMEM)
HBM = pl.BlockSpec(memory_space=pltpu.HBM)


def folded(part, momentum):
    return (part.astype(jnp.float32) + FOLD * momentum).astype(jnp.bfloat16)


def count_slots(owners_ref, first_ref, rank_ref):
    groups = first_ref.shape[0]
    for group in range(groups):
        first_ref[group] = 0
    for block in range(owners_ref.shape[0]):
        owner = owners_ref[block]
        slot = first_ref[owner]
        rank_ref[block] = slot
        first_ref[owner] = slot + 1
    first = jnp.int32(0)
    for group in range(groups):
        after = first + first_ref[group]
        first_ref[group] = first
        first = after


def split_rank(groups, rank):
    return rank & (groups - 1), rank >> (groups.bit_length() - 1)


def fold_kernel(
    groups,
    here_ref,
    owners_hbm,
    part_hbm,
    momentum_hbm,
    out_ref,
    owners_ref,
    first_ref,
    target_ref,
    owned_ref,
    part_ref,
    momentum_ref,
    sems,
):
    blocks, most = part_ref.shape[0], momentum_ref.shape[0]
    per_group = blocks // groups
    copies = [
        pltpu.make_async_copy(source, target, sems.at[index])
        for index, (source, target) in enumerate(
            [(owners_hbm, owners_ref), (part_hbm, part_ref), (momentum_hbm, momentum_ref)]
        )
    ]
    for copy in copies:
        copy.start()
    here = here_ref[0]
    copies[0].wait()
    count_slots(owners_ref, first_ref, target_ref)
    count = jnp.int32(0)
    for block in range(blocks):
        owner, slot = owners_ref[block], target_ref[block]
        mine = owner == here
        count = count + mine.astype(jnp.int32)
        owned_ref[jnp.where(mine, slot, most)] = block
        group, place = split_rank(groups, first_ref[owner] + slot)
        target_ref[block] = ((group - FIRST_GROUP) & (groups - 1)) * per_group + place
    copies[1].wait()
    for block in range(blocks):
        out_ref[target_ref[block]] = part_ref[block]
    copies[2].wait()
    for slot in range(most):

        @pl.when(slot < count)
        def _():
            block = owned_ref[slot]
            out_ref[target_ref[block]] = folded(part_ref[block], momentum_ref[slot])


def sums_kernel(
    groups, here_ref, owners_ref, total_ref, out_ref, first_out_ref, rank_out_ref, first_ref, rank_ref, sems
):
    per_group = total_ref.shape[0]
    count_slots(owners_ref, first_ref, rank_ref)
    for block in range(owners_ref.shape[0]):
        rank_ref[block] = first_ref[owners_ref[block]] + rank_ref[block]
    copies = [
        pltpu.make_async_copy(source, target, sems.at[index])
        for index, (source, target) in enumerate([(first_ref, first_out_ref), (rank_ref, rank_out_ref)])
    ]
    for copy in copies:
        copy.start()
    value = total_ref[0]
    for target in range(groups):
        out_ref[target, per_group] = value
    for place in range(per_group):
        rank = place * groups + here_ref[0]
        owner = jnp.int32(-1)
        for group in range(groups):
            owner = owner + (first_ref[group] <= rank).astype(jnp.int32)
        out_ref[owner, per_group] = total_ref[place]
    for copy in copies:
        copy.wait()


def sum_kernel(ring, parts_ref, send_ref, total_ref):
    count, blocks = parts_ref.shape[:2]
    for block in range(blocks):
        total = parts_ref[0, block].astype(jnp.float32)
        for source in range(1, count):
            total = total + parts_ref[source, block].astype(jnp.float32)
        total_ref[block] = total.astype(jnp.bfloat16)
        direction = (DIRECTION_SCALE * total).astype(jnp.bfloat16)
        for target, chip in enumerate(ring):
            if min(chip % SEGMENT, blocks - 1) == block:
                send_ref[target] = direction


def dot_nt(a, b):
    return lax.dot_general(a, b, (((1,), (1,)), ((), ())), preferred_element_type=jnp.float32)


def dot_nn(a, b):
    return jnp.dot(a, b, preferred_element_type=jnp.float32)


def newton_schulz_kernel(first_ref, own_ref, other_ref, out_ref, x_ref, y_ref, gram_ref, poly_ref):
    half, order = own_ref.shape
    kept = out_ref.shape[0]
    x_ref[0:half] = own_ref[...]
    x_ref[half:order] = other_ref[...]
    squares = jnp.zeros((8, order), jnp.float32)
    for ref in (own_ref, other_ref):
        wide = ref[...].astype(jnp.float32)
        squares = squares + jnp.sum((wide * wide).reshape(half // 8, 8, order), axis=0)
    inverse = 1.0 / (jnp.sqrt(jnp.sum(squares)) + EPSILON)
    source_ref, target_ref = x_ref, y_ref
    for iteration in range(NS_ITERS):
        gram = dot_nt(source_ref[...], source_ref[...])
        if iteration == 0:
            gram = gram * (inverse * inverse)
        gram_ref[...] = gram.astype(jnp.bfloat16)
        last = iteration == NS_ITERS - 1
        rows = pl.ds(pl.multiple_of(first_ref[0] * kept, kept), kept) if last else pl.ds(0, order)
        gram = gram_ref[rows]
        poly = (COEF_B * gram.astype(jnp.float32) + COEF_C * dot_nn(gram, gram_ref[...])).astype(jnp.bfloat16)
        if not last:
            poly_ref[...] = poly
            poly = poly_ref[...]
        fresh = COEF_A * source_ref[rows].astype(jnp.float32) + dot_nn(poly, source_ref[...])
        if iteration == 0:
            fresh = fresh * inverse
        if last:
            each = kept // SEGMENT
            for target, chip in enumerate(SEGMENT_ORDER):
                start = (SEGMENT - 1 - chip) * each
                out_ref[target * each : (target + 1) * each] = fresh[start : start + each].astype(jnp.bfloat16)
        else:
            target_ref[...] = fresh.astype(jnp.bfloat16)
            source_ref, target_ref = target_ref, source_ref


def spread_kernel(returned_ref, sums_ref, out_ref):
    del sums_ref
    for place in range(out_ref.shape[1] - 1):
        value = returned_ref[SEGMENT_ORDER.index(place)]
        for target in range(out_ref.shape[0]):
            out_ref[target, place] = value


def update_kernel(
    groups,
    scale,
    here_ref,
    first_ref,
    rank_ref,
    both_ref,
    weight_ref,
    part_ref,
    momentum_ref,
    step_hbm,
    new_hbm,
    moved_hbm,
    owned_ref,
    step_ref,
    new_ref,
    moved_ref,
    sems,
    moved_sem,
):
    blocks, most = weight_ref.shape[0], momentum_ref.shape[0]
    per_group = blocks // groups
    each = blocks // PIECES
    leaving = []

    def leave(source, target, sem):
        leaving.append(pltpu.make_async_copy(source, target, sem))
        leaving[-1].start()

    for index in range(PIECES):
        chunk = pl.ds(index * each, each)
        for block in range(index * each, (index + 1) * each):
            group, place = split_rank(groups, rank_ref[block])
            step = both_ref[group, place].astype(jnp.float32) * scale
            step_ref[block] = step
            new_ref[block] = weight_ref[block] - LEARN_RATE * step
        leave(step_ref.at[chunk], step_hbm.at[chunk], sems.at[index, 0])
        leave(new_ref.at[chunk], new_hbm.at[chunk], sems.at[index, 1])
    here = here_ref[0]
    first = first_ref[here]
    after = jnp.where(here == groups - 1, blocks, first_ref[jnp.minimum(here + 1, groups - 1)])
    count = after - first
    for block in range(blocks):
        slot = rank_ref[block] - first
        owned_ref[jnp.where((slot >= 0) & (slot < count), slot, most)] = block
    for slot in range(most):
        used = slot < count
        block = jnp.where(used, owned_ref[slot], 0)
        group, _ = split_rank(groups, first + slot)
        part = part_ref[block]
        before = momentum_ref[slot]
        added = folded(part, before).astype(jnp.float32) - part.astype(jnp.float32)
        gradient = both_ref[group, per_group].astype(jnp.float32) - added
        moved_ref[slot] = jnp.where(used, MOMENTUM_DECAY * before + gradient, before)
    leave(moved_ref, moved_hbm, moved_sem)
    for copy in leaving:
        copy.wait()


def call(kernel, out_shape, in_specs, scratch=(), flops=0, moved=0, out_specs=None, room=40.0, aliases={}):
    return pl.pallas_call(
        kernel,
        out_shape=out_shape,
        in_specs=in_specs,
        out_specs=jax.tree.map(lambda _: VMEM, out_shape) if out_specs is None else out_specs,
        scratch_shapes=list(scratch),
        input_output_aliases=aliases,
        compiler_params=pltpu.CompilerParams(vmem_limit_bytes=int((64 - room) * 1024 * 1024)),
        cost_estimate=pl.CostEstimate(flops=flops, bytes_accessed=moved, transcendentals=0),
    )


def on_device(grad_parts, momentum, weight, owners):
    part = grad_parts[0]
    blocks, rows, order = part.shape
    most = momentum.shape[0]
    groups = lax.axis_size("rep")
    members = lax.axis_size("fsdp")
    chips = members // 2
    per_group = blocks // groups
    bf16 = functools.partial(jax.ShapeDtypeStruct, dtype=jnp.bfloat16)
    f32 = functools.partial(jax.ShapeDtypeStruct, dtype=jnp.float32)
    here = lax.axis_index("rep").astype(jnp.int32).reshape(1)
    segments = chips // SEGMENT
    ring = [(SEGMENT * TOP_SEGMENTS - 1 - index) % chips for index in range(chips)]
    same_core = [[2 * chip + core for chip in ring] for core in range(2)]
    same_segment = [
        [2 * (SEGMENT * s + chip) + core for chip in SEGMENT_ORDER] for s in range(segments) for core in range(2)
    ]
    from_first = [[(FIRST_GROUP + index) % groups for index in range(groups)]]
    segment = lax.axis_index("fsdp") // (2 * SEGMENT)
    listed = lax.rem(TOP_SEGMENTS - 1 + segments - segment, segments).astype(jnp.int32).reshape(1)

    with jax.named_scope("fold_momentum"):
        parts = call(
            functools.partial(fold_kernel, groups),
            pltpu.VMEM((blocks, rows, order), jnp.bfloat16),
            [SMEM, HBM, HBM, HBM],
            [
                pltpu.SMEM((blocks,), jnp.int32),
                pltpu.SMEM((groups,), jnp.int32),
                pltpu.SMEM((blocks,), jnp.int32),
                pltpu.SMEM((most + 1,), jnp.int32),
                pltpu.VMEM(part.shape, jnp.bfloat16),
                pltpu.VMEM(momentum.shape, jnp.float32),
                pltpu.SemaphoreType.DMA((3,)),
            ],
            moved=1 << 21,
        )(here, *(pltpu.with_memory_space_constraint(array, pltpu.HBM) for array in (owners, part, momentum)))
    with jax.named_scope("reduce_over_rep"):
        received = lax.all_to_all(
            parts.reshape(groups, per_group, rows, order),
            "rep",
            0,
            0,
            axis_index_groups=from_first,
            tiled=True,
        )
        send, total = call(
            functools.partial(sum_kernel, ring),
            [bf16((chips, rows, order)), bf16((per_group, rows, order))],
            [VMEM],
            moved=1 << 20,
        )(received)
    with jax.named_scope("gather_rows"):
        own = lax.all_to_all(send, "fsdp", 0, 0, axis_index_groups=same_core, tiled=True)
        own = own.reshape(chips * rows, order)
        other = lax.ppermute(own, "fsdp", [(i, i ^ 1) for i in range(members)])
    with jax.named_scope("sums_to_owners"):
        late_owners, own = lax.optimization_barrier((owners, own))
        sums, first, ranks = call(
            functools.partial(sums_kernel, groups),
            [
                pltpu.VMEM((groups, per_group + 1, rows, order), jnp.bfloat16),
                pltpu.VMEM((groups,), jnp.int32),
                pltpu.VMEM((blocks,), jnp.int32),
            ],
            [SMEM, SMEM, VMEM],
            [
                pltpu.SMEM((groups,), jnp.int32),
                pltpu.SMEM((blocks,), jnp.int32),
                pltpu.SemaphoreType.DMA((2,)),
            ],
            moved=1 << 20,
        )(here, late_owners, total)
        other, ranks = lax.optimization_barrier((other, ranks))
    with jax.named_scope("orthogonalize"):
        square = pltpu.VMEM((order, order), jnp.bfloat16)
        kept = call(
            newton_schulz_kernel,
            bf16((SEGMENT * rows, order)),
            [SMEM, VMEM, VMEM],
            [square] * 4,
            flops=15 * order**3,
            moved=1 << 20,
        )(listed, own, other)
    with jax.named_scope("return_rows"):
        returned = lax.all_to_all(
            kept.reshape(SEGMENT, rows, order), "fsdp", 0, 0, axis_index_groups=same_segment, tiled=True
        )
        spread = call(
            spread_kernel,
            bf16(sums.shape),
            [VMEM, VMEM],
            moved=1 << 20,
            aliases={1: 0},
        )(returned, sums)
        both = lax.all_to_all(spread, "rep", 0, 0, tiled=True)
    with jax.named_scope("update"):
        return call(
            functools.partial(update_kernel, groups, 0.2 * math.sqrt(order)),
            [f32(weight.shape), f32(weight.shape), f32(momentum.shape)],
            [SMEM, SMEM, SMEM, VMEM, VMEM, VMEM, VMEM],
            [
                pltpu.SMEM((most + 1,), jnp.int32),
                pltpu.VMEM(weight.shape, jnp.float32),
                pltpu.VMEM(weight.shape, jnp.float32),
                pltpu.VMEM(momentum.shape, jnp.float32),
                pltpu.SemaphoreType.DMA((PIECES, 2)),
                pltpu.SemaphoreType.DMA,
            ],
            moved=5 << 20,
            out_specs=[HBM, HBM, HBM],
        )(here, first, ranks, both, weight, part, momentum)


def solution(mesh):
    return jax.shard_map(
        on_device,
        mesh=mesh,
        in_specs=(P("rep", None, "fsdp", None), P("rep", "fsdp", None), P(None, "fsdp", None), P()),
        out_specs=(P(None, "fsdp", None), P(None, "fsdp", None), P("rep", "fsdp", None)),
        check_vma=False,
    )
```

```python
import functools
import math

import jax
import jax.numpy as jnp
from jax import lax
from jax.experimental import pallas as pl
from jax.experimental.pallas import tpu as pltpu
from jax.sharding import PartitionSpec as P

NS_ITERS = 3
COEF_A = 3.4445
COEF_B = -4.775
COEF_C = 2.0315
MOMENTUM_DECAY = 0.95
LEARN_RATE = 0.02
EPSILON = 1e-07
DIRECTION_SCALE = 1.0 + MOMENTUM_DECAY
FOLD = MOMENTUM_DECAY * MOMENTUM_DECAY / DIRECTION_SCALE
SEGMENT = 4
PIECES = 6
FIRST_GROUP = 14
TOP_SEGMENTS = 3
SEGMENT_ORDER = (2, 1, 3, 0)

VMEM = pl.BlockSpec(memory_space=pltpu.VMEM)
SMEM = pl.BlockSpec(memory_space=pltpu.SMEM)
HBM = pl.BlockSpec(memory_space=pltpu.HBM)


def folded(part, momentum):
    return (part.astype(jnp.float32) + FOLD * momentum).astype(jnp.bfloat16)


def count_slots(owners_ref, first_ref, rank_ref):
    groups = first_ref.shape[0]
    for group in range(groups):
        first_ref[group] = 0
    for block in range(owners_ref.shape[0]):
        owner = owners_ref[block]
        slot = first_ref[owner]
        rank_ref[block] = slot
        first_ref[owner] = slot + 1
    first = jnp.int32(0)
    for group in range(groups):
        after = first + first_ref[group]
        first_ref[group] = first
        first = after


def split_rank(groups, rank):
    return rank & (groups - 1), rank >> (groups.bit_length() - 1)


def fold_kernel(
    groups,
    here_ref,
    owners_hbm,
    part_hbm,
    momentum_hbm,
    out_ref,
    owners_ref,
    first_ref,
    target_ref,
    owned_ref,
    part_ref,
    momentum_ref,
    sems,
):
    blocks, most = part_ref.shape[0], momentum_ref.shape[0]
    per_group = blocks // groups
    copies = [
        pltpu.make_async_copy(source, target, sems.at[index])
        for index, (source, target) in enumerate(
            [(owners_hbm, owners_ref), (part_hbm, part_ref), (momentum_hbm, momentum_ref)]
        )
    ]
    for copy in copies:
        copy.start()
    here = here_ref[0]
    copies[0].wait()
    count_slots(owners_ref, first_ref, target_ref)
    count = jnp.int32(0)
    for block in range(blocks):
        owner, slot = owners_ref[block], target_ref[block]
        mine = owner == here
        count = count + mine.astype(jnp.int32)
        owned_ref[jnp.where(mine, slot, most)] = block
        group, place = split_rank(groups, first_ref[owner] + slot)
        target_ref[block] = ((group - FIRST_GROUP) & (groups - 1)) * per_group + place
    copies[1].wait()
    for block in range(blocks):
        out_ref[target_ref[block]] = part_ref[block]
    copies[2].wait()
    for slot in range(most):

        @pl.when(slot < count)
        def _():
            block = owned_ref[slot]
            out_ref[target_ref[block]] = folded(part_ref[block], momentum_ref[slot])


def sums_kernel(
    groups, here_ref, owners_ref, total_ref, out_ref, first_out_ref, rank_out_ref, first_ref, rank_ref, sems
):
    per_group = total_ref.shape[0]
    count_slots(owners_ref, first_ref, rank_ref)
    for block in range(owners_ref.shape[0]):
        rank_ref[block] = first_ref[owners_ref[block]] + rank_ref[block]
    copies = [
        pltpu.make_async_copy(source, target, sems.at[index])
        for index, (source, target) in enumerate([(first_ref, first_out_ref), (rank_ref, rank_out_ref)])
    ]
    for copy in copies:
        copy.start()
    value = total_ref[0]
    for target in range(groups):
        out_ref[target] = value
    for place in range(per_group):
        rank = place * groups + here_ref[0]
        owner = jnp.int32(-1)
        for group in range(groups):
            owner = owner + (first_ref[group] <= rank).astype(jnp.int32)
        out_ref[owner] = total_ref[place]
    for copy in copies:
        copy.wait()


def sum_kernel(ring, parts_ref, send_ref, total_ref):
    count, blocks = parts_ref.shape[:2]
    for block in range(blocks):
        total = parts_ref[0, block].astype(jnp.float32)
        for source in range(1, count):
            total = total + parts_ref[source, block].astype(jnp.float32)
        total_ref[block] = total.astype(jnp.bfloat16)
        direction = (DIRECTION_SCALE * total).astype(jnp.bfloat16)
        for target, chip in enumerate(ring):
            if min(chip % SEGMENT, blocks - 1) == block:
                send_ref[target] = direction


def dot_nt(a, b):
    return lax.dot_general(a, b, (((1,), (1,)), ((), ())), preferred_element_type=jnp.float32)


def dot_nn(a, b):
    return jnp.dot(a, b, preferred_element_type=jnp.float32)


def newton_schulz_kernel(first_ref, own_ref, other_ref, out_ref, x_ref, y_ref, gram_ref, poly_ref):
    half, order = own_ref.shape
    kept = out_ref.shape[0]
    x_ref[0:half] = own_ref[...]
    x_ref[half:order] = other_ref[...]
    squares = jnp.zeros((8, order), jnp.float32)
    for ref in (own_ref, other_ref):
        wide = ref[...].astype(jnp.float32)
        squares = squares + jnp.sum((wide * wide).reshape(half // 8, 8, order), axis=0)
    inverse = 1.0 / (jnp.sqrt(jnp.sum(squares)) + EPSILON)
    source_ref, target_ref = x_ref, y_ref
    for iteration in range(NS_ITERS):
        gram = dot_nt(source_ref[...], source_ref[...])
        if iteration == 0:
            gram = gram * (inverse * inverse)
        gram_ref[...] = gram.astype(jnp.bfloat16)
        last = iteration == NS_ITERS - 1
        rows = pl.ds(pl.multiple_of(first_ref[0] * kept, kept), kept) if last else pl.ds(0, order)
        gram = gram_ref[rows]
        poly = (COEF_B * gram.astype(jnp.float32) + COEF_C * dot_nn(gram, gram_ref[...])).astype(jnp.bfloat16)
        if not last:
            poly_ref[...] = poly
            poly = poly_ref[...]
        fresh = COEF_A * source_ref[rows].astype(jnp.float32) + dot_nn(poly, source_ref[...])
        if iteration == 0:
            fresh = fresh * inverse
        if last:
            each = kept // SEGMENT
            for target, chip in enumerate(SEGMENT_ORDER):
                start = (SEGMENT - 1 - chip) * each
                out_ref[target * each : (target + 1) * each] = fresh[start : start + each].astype(jnp.bfloat16)
        else:
            target_ref[...] = fresh.astype(jnp.bfloat16)
            source_ref, target_ref = target_ref, source_ref


def spread_kernel(returned_ref, sums_ref, out_ref):
    per_group = out_ref.shape[1] - 1
    for target in range(out_ref.shape[0]):
        out_ref[target, per_group] = sums_ref[target]
    for place in range(per_group):
        value = returned_ref[SEGMENT_ORDER.index(place)]
        for target in range(out_ref.shape[0]):
            out_ref[target, place] = value


def update_kernel(
    groups,
    scale,
    here_ref,
    first_ref,
    rank_ref,
    both_ref,
    weight_ref,
    part_ref,
    momentum_ref,
    step_hbm,
    new_hbm,
    moved_hbm,
    owned_ref,
    step_ref,
    new_ref,
    moved_ref,
    sems,
    moved_sem,
):
    blocks, most = weight_ref.shape[0], momentum_ref.shape[0]
    per_group = blocks // groups
    each = blocks // PIECES
    leaving = []

    def leave(source, target, sem):
        leaving.append(pltpu.make_async_copy(source, target, sem))
        leaving[-1].start()

    for index in range(PIECES):
        chunk = pl.ds(index * each, each)
        for block in range(index * each, (index + 1) * each):
            group, place = split_rank(groups, rank_ref[block])
            step = both_ref[group, place].astype(jnp.float32) * scale
            step_ref[block] = step
            new_ref[block] = weight_ref[block] - LEARN_RATE * step
        leave(step_ref.at[chunk], step_hbm.at[chunk], sems.at[index, 0])
        leave(new_ref.at[chunk], new_hbm.at[chunk], sems.at[index, 1])
    here = here_ref[0]
    first = first_ref[here]
    after = jnp.where(here == groups - 1, blocks, first_ref[jnp.minimum(here + 1, groups - 1)])
    count = after - first
    for block in range(blocks):
        slot = rank_ref[block] - first
        owned_ref[jnp.where((slot >= 0) & (slot < count), slot, most)] = block
    for slot in range(most):
        used = slot < count
        block = jnp.where(used, owned_ref[slot], 0)
        group, _ = split_rank(groups, first + slot)
        part = part_ref[block]
        before = momentum_ref[slot]
        added = folded(part, before).astype(jnp.float32) - part.astype(jnp.float32)
        gradient = both_ref[group, per_group].astype(jnp.float32) - added
        moved_ref[slot] = jnp.where(used, MOMENTUM_DECAY * before + gradient, before)
    leave(moved_ref, moved_hbm, moved_sem)
    for copy in leaving:
        copy.wait()


def call(kernel, out_shape, in_specs, scratch=(), flops=0, moved=0, out_specs=None):
    return pl.pallas_call(
        kernel,
        out_shape=out_shape,
        in_specs=in_specs,
        out_specs=jax.tree.map(lambda _: VMEM, out_shape) if out_specs is None else out_specs,
        scratch_shapes=list(scratch),
        compiler_params=pltpu.CompilerParams(vmem_limit_bytes=24 * 1024 * 1024),
        cost_estimate=pl.CostEstimate(flops=flops, bytes_accessed=moved, transcendentals=0),
    )


def on_device(grad_parts, momentum, weight, owners):
    part = grad_parts[0]
    blocks, rows, order = part.shape
    most = momentum.shape[0]
    groups = lax.axis_size("rep")
    members = lax.axis_size("fsdp")
    chips = members // 2
    per_group = blocks // groups
    bf16 = functools.partial(jax.ShapeDtypeStruct, dtype=jnp.bfloat16)
    f32 = functools.partial(jax.ShapeDtypeStruct, dtype=jnp.float32)
    here = lax.axis_index("rep").astype(jnp.int32).reshape(1)
    segments = chips // SEGMENT
    ring = [(SEGMENT * TOP_SEGMENTS - 1 - index) % chips for index in range(chips)]
    same_core = [[2 * chip + core for chip in ring] for core in range(2)]
    same_segment = [
        [2 * (SEGMENT * s + chip) + core for chip in SEGMENT_ORDER] for s in range(segments) for core in range(2)
    ]
    from_first = [[(FIRST_GROUP + index) % groups for index in range(groups)]]
    segment = lax.axis_index("fsdp") // (2 * SEGMENT)
    listed = lax.rem(TOP_SEGMENTS - 1 + segments - segment, segments).astype(jnp.int32).reshape(1)

    with jax.named_scope("fold_momentum"):
        parts = call(
            functools.partial(fold_kernel, groups),
            pltpu.VMEM((blocks, rows, order), jnp.bfloat16),
            [SMEM, HBM, HBM, HBM],
            [
                pltpu.SMEM((blocks,), jnp.int32),
                pltpu.SMEM((groups,), jnp.int32),
                pltpu.SMEM((blocks,), jnp.int32),
                pltpu.SMEM((most + 1,), jnp.int32),
                pltpu.VMEM(part.shape, jnp.bfloat16),
                pltpu.VMEM(momentum.shape, jnp.float32),
                pltpu.SemaphoreType.DMA((3,)),
            ],
            moved=1 << 21,
        )(here, *(pltpu.with_memory_space_constraint(array, pltpu.HBM) for array in (owners, part, momentum)))
    with jax.named_scope("reduce_over_rep"):
        received = lax.all_to_all(
            parts.reshape(groups, per_group, rows, order),
            "rep",
            0,
            0,
            axis_index_groups=from_first,
            tiled=True,
        )
        send, total = call(
            functools.partial(sum_kernel, ring),
            [bf16((chips, rows, order)), bf16((per_group, rows, order))],
            [VMEM],
            moved=1 << 20,
        )(received)
    with jax.named_scope("gather_rows"):
        own = lax.all_to_all(send, "fsdp", 0, 0, axis_index_groups=same_core, tiled=True)
        own = own.reshape(chips * rows, order)
        other = lax.ppermute(own, "fsdp", [(i, i ^ 1) for i in range(members)])
    with jax.named_scope("sums_to_owners"):
        late_owners, own = lax.optimization_barrier((owners, own))
        sums, first, ranks = call(
            functools.partial(sums_kernel, groups),
            [
                pltpu.VMEM((groups, rows, order), jnp.bfloat16),
                pltpu.VMEM((groups,), jnp.int32),
                pltpu.VMEM((blocks,), jnp.int32),
            ],
            [SMEM, SMEM, VMEM],
            [
                pltpu.SMEM((groups,), jnp.int32),
                pltpu.SMEM((blocks,), jnp.int32),
                pltpu.SemaphoreType.DMA((2,)),
            ],
            moved=1 << 20,
        )(here, late_owners, total)
        other, ranks = lax.optimization_barrier((other, ranks))
    with jax.named_scope("orthogonalize"):
        square = pltpu.VMEM((order, order), jnp.bfloat16)
        kept = call(
            newton_schulz_kernel,
            bf16((SEGMENT * rows, order)),
            [SMEM, VMEM, VMEM],
            [square] * 4,
            flops=15 * order**3,
            moved=1 << 20,
        )(listed, own, other)
    with jax.named_scope("return_rows"):
        returned = lax.all_to_all(
            kept.reshape(SEGMENT, rows, order), "fsdp", 0, 0, axis_index_groups=same_segment, tiled=True
        )
        spread = call(
            spread_kernel,
            bf16((groups, per_group + 1, rows, order)),
            [VMEM, VMEM],
            moved=1 << 20,
        )(returned, sums)
        both = lax.all_to_all(spread, "rep", 0, 0, tiled=True)
    with jax.named_scope("update"):
        return call(
            functools.partial(update_kernel, groups, 0.2 * math.sqrt(order)),
            [f32(weight.shape), f32(weight.shape), f32(momentum.shape)],
            [SMEM, SMEM, SMEM, VMEM, VMEM, VMEM, VMEM],
            [
                pltpu.SMEM((most + 1,), jnp.int32),
                pltpu.VMEM(weight.shape, jnp.float32),
                pltpu.VMEM(weight.shape, jnp.float32),
                pltpu.VMEM(momentum.shape, jnp.float32),
                pltpu.SemaphoreType.DMA((PIECES, 2)),
                pltpu.SemaphoreType.DMA,
            ],
            moved=5 << 20,
            out_specs=[HBM, HBM, HBM],
        )(here, first, ranks, both, weight, part, momentum)


def solution(mesh):
    return jax.shard_map(
        on_device,
        mesh=mesh,
        in_specs=(P("rep", None, "fsdp", None), P("rep", "fsdp", None), P(None, "fsdp", None), P()),
        out_specs=(P(None, "fsdp", None), P(None, "fsdp", None), P("rep", "fsdp", None)),
        check_vma=False,
    )
```

```python
import functools
import math

import jax
import jax.numpy as jnp
from jax import lax
from jax.experimental import pallas as pl
from jax.experimental.pallas import tpu as pltpu
from jax.sharding import PartitionSpec as P

NS_ITERS = 3
COEF_A = 3.4445
COEF_B = -4.775
COEF_C = 2.0315
MOMENTUM_DECAY = 0.95
LEARN_RATE = 0.02
EPSILON = 1e-07
DIRECTION_SCALE = 1.0 + MOMENTUM_DECAY
FOLD = MOMENTUM_DECAY * MOMENTUM_DECAY / DIRECTION_SCALE
SEGMENT = 4
PIECES = 6
FIRST_GROUP = 14
TOP_SEGMENTS = 3
SEGMENT_ORDER = (2, 1, 3, 0)

VMEM = pl.BlockSpec(memory_space=pltpu.VMEM)
SMEM = pl.BlockSpec(memory_space=pltpu.SMEM)
HBM = pl.BlockSpec(memory_space=pltpu.HBM)


def folded(part, momentum):
    return (part.astype(jnp.float32) + FOLD * momentum).astype(jnp.bfloat16)


def count_slots(owners_ref, first_ref, slot_ref):
    groups = first_ref.shape[0]
    for group in range(groups):
        first_ref[group] = 0
    for block in range(owners_ref.shape[0]):
        owner = owners_ref[block]
        slot = first_ref[owner]
        slot_ref[block] = slot
        first_ref[owner] = slot + 1
    first = jnp.int32(0)
    for group in range(groups):
        after = first + first_ref[group]
        first_ref[group] = first
        first = after


def split_rank(groups, rank):
    return rank & (groups - 1), rank >> (groups.bit_length() - 1)


def fold_kernel(
    groups,
    here_ref,
    owners_hbm,
    part_hbm,
    momentum_hbm,
    out_ref,
    owners_ref,
    first_ref,
    target_ref,
    owned_ref,
    part_ref,
    momentum_ref,
    sems,
):
    blocks, most = part_ref.shape[0], momentum_ref.shape[0]
    per_group = blocks // groups
    copies = [
        pltpu.make_async_copy(source, target, sems.at[index])
        for index, (source, target) in enumerate(
            [(owners_hbm, owners_ref), (part_hbm, part_ref), (momentum_hbm, momentum_ref)]
        )
    ]
    for copy in copies:
        copy.start()
    here = here_ref[0]
    copies[0].wait()
    count_slots(owners_ref, first_ref, target_ref)
    count = jnp.int32(0)
    for block in range(blocks):
        owner, slot = owners_ref[block], target_ref[block]
        mine = owner == here
        count = count + mine.astype(jnp.int32)
        owned_ref[jnp.where(mine, slot, most)] = block
        group, place = split_rank(groups, first_ref[owner] + slot)
        target_ref[block] = ((group - FIRST_GROUP) & (groups - 1)) * per_group + place
    copies[1].wait()
    for block in range(blocks):
        out_ref[target_ref[block]] = part_ref[block]
    copies[2].wait()
    for slot in range(most):

        @pl.when(slot < count)
        def _():
            block = owned_ref[slot]
            out_ref[target_ref[block]] = folded(part_ref[block], momentum_ref[slot])


def sums_kernel(
    groups, here_ref, owners_ref, total_ref, out_ref, first_out_ref, slot_out_ref, first_ref, slot_ref, sems
):
    per_group = total_ref.shape[0]
    count_slots(owners_ref, first_ref, slot_ref)
    copies = [
        pltpu.make_async_copy(source, target, sems.at[index])
        for index, (source, target) in enumerate([(first_ref, first_out_ref), (slot_ref, slot_out_ref)])
    ]
    for copy in copies:
        copy.start()
    value = total_ref[0]
    for target in range(groups):
        out_ref[target] = value
    for place in range(per_group):
        rank = place * groups + here_ref[0]
        owner = jnp.int32(-1)
        for group in range(groups):
            owner = owner + (first_ref[group] <= rank).astype(jnp.int32)
        out_ref[owner] = total_ref[place]
    for copy in copies:
        copy.wait()


def sum_kernel(ring, parts_ref, send_ref, total_ref):
    count, blocks = parts_ref.shape[:2]
    for block in range(blocks):
        total = parts_ref[0, block].astype(jnp.float32)
        for source in range(1, count):
            total = total + parts_ref[source, block].astype(jnp.float32)
        total_ref[block] = total.astype(jnp.bfloat16)
        direction = (DIRECTION_SCALE * total).astype(jnp.bfloat16)
        for target, chip in enumerate(ring):
            if min(chip % SEGMENT, blocks - 1) == block:
                send_ref[target] = direction


def dot_nt(a, b):
    return lax.dot_general(a, b, (((1,), (1,)), ((), ())), preferred_element_type=jnp.float32)


def dot_nn(a, b):
    return jnp.dot(a, b, preferred_element_type=jnp.float32)


def newton_schulz_kernel(first_ref, own_ref, other_ref, out_ref, x_ref, y_ref, gram_ref, poly_ref):
    half, order = own_ref.shape
    kept = out_ref.shape[0]
    x_ref[0:half] = own_ref[...]
    x_ref[half:order] = other_ref[...]
    squares = jnp.zeros((8, order), jnp.float32)
    for ref in (own_ref, other_ref):
        wide = ref[...].astype(jnp.float32)
        squares = squares + jnp.sum((wide * wide).reshape(half // 8, 8, order), axis=0)
    inverse = 1.0 / (jnp.sqrt(jnp.sum(squares)) + EPSILON)
    source_ref, target_ref = x_ref, y_ref
    for iteration in range(NS_ITERS):
        gram = dot_nt(source_ref[...], source_ref[...])
        if iteration == 0:
            gram = gram * (inverse * inverse)
        gram_ref[...] = gram.astype(jnp.bfloat16)
        last = iteration == NS_ITERS - 1
        rows = pl.ds(pl.multiple_of(first_ref[0] * kept, kept), kept) if last else pl.ds(0, order)
        gram = gram_ref[rows]
        poly = (COEF_B * gram.astype(jnp.float32) + COEF_C * dot_nn(gram, gram_ref[...])).astype(jnp.bfloat16)
        if not last:
            poly_ref[...] = poly
            poly = poly_ref[...]
        fresh = COEF_A * source_ref[rows].astype(jnp.float32) + dot_nn(poly, source_ref[...])
        if iteration == 0:
            fresh = fresh * inverse
        if last:
            each = kept // SEGMENT
            for target, chip in enumerate(SEGMENT_ORDER):
                start = (SEGMENT - 1 - chip) * each
                out_ref[target * each : (target + 1) * each] = fresh[start : start + each].astype(jnp.bfloat16)
        else:
            target_ref[...] = fresh.astype(jnp.bfloat16)
            source_ref, target_ref = target_ref, source_ref


def spread_kernel(returned_ref, sums_ref, out_ref):
    per_group = out_ref.shape[1] - 1
    for target in range(out_ref.shape[0]):
        out_ref[target, per_group] = sums_ref[target]
    for place in range(per_group):
        value = returned_ref[SEGMENT_ORDER.index(place)]
        for target in range(out_ref.shape[0]):
            out_ref[target, place] = value


def update_kernel(
    groups,
    scale,
    here_ref,
    owners_ref,
    first_ref,
    slot_ref,
    both_ref,
    weight_ref,
    part_ref,
    momentum_ref,
    step_hbm,
    new_hbm,
    moved_hbm,
    owned_ref,
    step_ref,
    new_ref,
    moved_ref,
    sems,
    moved_sem,
):
    blocks, most = weight_ref.shape[0], momentum_ref.shape[0]
    per_group = blocks // groups
    each = blocks // PIECES
    leaving = []

    def leave(source, target, sem):
        leaving.append(pltpu.make_async_copy(source, target, sem))
        leaving[-1].start()

    for index in range(PIECES):
        chunk = pl.ds(index * each, each)
        for block in range(index * each, (index + 1) * each):
            group, place = split_rank(groups, first_ref[owners_ref[block]] + slot_ref[block])
            step = both_ref[group, place].astype(jnp.float32) * scale
            step_ref[block] = step
            new_ref[block] = weight_ref[block] - LEARN_RATE * step
        leave(step_ref.at[chunk], step_hbm.at[chunk], sems.at[index, 0])
        leave(new_ref.at[chunk], new_hbm.at[chunk], sems.at[index, 1])
    here = here_ref[0]
    first = first_ref[here]
    count = jnp.int32(0)
    for block in range(blocks):
        mine = owners_ref[block] == here
        count = count + mine.astype(jnp.int32)
        owned_ref[jnp.where(mine, slot_ref[block], most)] = block
    for slot in range(most):
        used = slot < count
        block = jnp.where(used, owned_ref[slot], 0)
        group, _ = split_rank(groups, first + slot)
        part = part_ref[block]
        before = momentum_ref[slot]
        added = folded(part, before).astype(jnp.float32) - part.astype(jnp.float32)
        gradient = both_ref[group, per_group].astype(jnp.float32) - added
        moved_ref[slot] = jnp.where(used, MOMENTUM_DECAY * before + gradient, before)
    leave(moved_ref, moved_hbm, moved_sem)
    for copy in leaving:
        copy.wait()


def call(kernel, out_shape, in_specs, scratch=(), flops=0, moved=0, out_specs=None):
    return pl.pallas_call(
        kernel,
        out_shape=out_shape,
        in_specs=in_specs,
        out_specs=jax.tree.map(lambda _: VMEM, out_shape) if out_specs is None else out_specs,
        scratch_shapes=list(scratch),
        compiler_params=pltpu.CompilerParams(vmem_limit_bytes=24 * 1024 * 1024),
        cost_estimate=pl.CostEstimate(flops=flops, bytes_accessed=moved, transcendentals=0),
    )


def on_device(grad_parts, momentum, weight, owners):
    part = grad_parts[0]
    blocks, rows, order = part.shape
    most = momentum.shape[0]
    groups = lax.axis_size("rep")
    members = lax.axis_size("fsdp")
    chips = members // 2
    per_group = blocks // groups
    bf16 = functools.partial(jax.ShapeDtypeStruct, dtype=jnp.bfloat16)
    f32 = functools.partial(jax.ShapeDtypeStruct, dtype=jnp.float32)
    here = lax.axis_index("rep").astype(jnp.int32).reshape(1)
    segments = chips // SEGMENT
    ring = [(SEGMENT * TOP_SEGMENTS - 1 - index) % chips for index in range(chips)]
    same_core = [[2 * chip + core for chip in ring] for core in range(2)]
    same_segment = [
        [2 * (SEGMENT * s + chip) + core for chip in SEGMENT_ORDER] for s in range(segments) for core in range(2)
    ]
    from_first = [[(FIRST_GROUP + index) % groups for index in range(groups)]]
    segment = lax.axis_index("fsdp") // (2 * SEGMENT)
    listed = lax.rem(TOP_SEGMENTS - 1 + segments - segment, segments).astype(jnp.int32).reshape(1)

    with jax.named_scope("fold_momentum"):
        parts = call(
            functools.partial(fold_kernel, groups),
            pltpu.VMEM((blocks, rows, order), jnp.bfloat16),
            [SMEM, HBM, HBM, HBM],
            [
                pltpu.SMEM((blocks,), jnp.int32),
                pltpu.SMEM((groups,), jnp.int32),
                pltpu.SMEM((blocks,), jnp.int32),
                pltpu.SMEM((most + 1,), jnp.int32),
                pltpu.VMEM(part.shape, jnp.bfloat16),
                pltpu.VMEM(momentum.shape, jnp.float32),
                pltpu.SemaphoreType.DMA((3,)),
            ],
            moved=1 << 21,
        )(here, *(pltpu.with_memory_space_constraint(array, pltpu.HBM) for array in (owners, part, momentum)))
    with jax.named_scope("reduce_over_rep"):
        received = lax.all_to_all(
            parts.reshape(groups, per_group, rows, order),
            "rep",
            0,
            0,
            axis_index_groups=from_first,
            tiled=True,
        )
        send, total = call(
            functools.partial(sum_kernel, ring),
            [bf16((chips, rows, order)), bf16((per_group, rows, order))],
            [VMEM],
            moved=1 << 20,
        )(received)
    with jax.named_scope("gather_rows"):
        own = lax.all_to_all(send, "fsdp", 0, 0, axis_index_groups=same_core, tiled=True)
        own = own.reshape(chips * rows, order)
        other = lax.ppermute(own, "fsdp", [(i, i ^ 1) for i in range(members)])
    with jax.named_scope("sums_to_owners"):
        late_owners, own = lax.optimization_barrier((owners, own))
        sums, first, slots = call(
            functools.partial(sums_kernel, groups),
            [
                pltpu.VMEM((groups, rows, order), jnp.bfloat16),
                pltpu.VMEM((groups,), jnp.int32),
                pltpu.VMEM((blocks,), jnp.int32),
            ],
            [SMEM, SMEM, VMEM],
            [
                pltpu.SMEM((groups,), jnp.int32),
                pltpu.SMEM((blocks,), jnp.int32),
                pltpu.SemaphoreType.DMA((2,)),
            ],
            moved=1 << 20,
        )(here, late_owners, total)
        other, slots = lax.optimization_barrier((other, slots))
    with jax.named_scope("orthogonalize"):
        square = pltpu.VMEM((order, order), jnp.bfloat16)
        kept = call(
            newton_schulz_kernel,
            bf16((SEGMENT * rows, order)),
            [SMEM, VMEM, VMEM],
            [square] * 4,
            flops=15 * order**3,
            moved=1 << 20,
        )(listed, own, other)
    with jax.named_scope("return_rows"):
        returned = lax.all_to_all(
            kept.reshape(SEGMENT, rows, order), "fsdp", 0, 0, axis_index_groups=same_segment, tiled=True
        )
        spread = call(
            spread_kernel,
            bf16((groups, per_group + 1, rows, order)),
            [VMEM, VMEM],
            moved=1 << 20,
        )(returned, sums)
        both = lax.all_to_all(spread, "rep", 0, 0, tiled=True)
    with jax.named_scope("update"):
        return call(
            functools.partial(update_kernel, groups, 0.2 * math.sqrt(order)),
            [f32(weight.shape), f32(weight.shape), f32(momentum.shape)],
            [SMEM, SMEM, SMEM, SMEM, VMEM, VMEM, VMEM, VMEM],
            [
                pltpu.SMEM((most + 1,), jnp.int32),
                pltpu.VMEM(weight.shape, jnp.float32),
                pltpu.VMEM(weight.shape, jnp.float32),
                pltpu.VMEM(momentum.shape, jnp.float32),
                pltpu.SemaphoreType.DMA((PIECES, 2)),
                pltpu.SemaphoreType.DMA,
            ],
            moved=5 << 20,
            out_specs=[HBM, HBM, HBM],
        )(here, late_owners, first, slots, both, weight, part, momentum)


def solution(mesh):
    return jax.shard_map(
        on_device,
        mesh=mesh,
        in_specs=(P("rep", None, "fsdp", None), P("rep", "fsdp", None), P(None, "fsdp", None), P()),
        out_specs=(P(None, "fsdp", None), P(None, "fsdp", None), P("rep", "fsdp", None)),
        check_vma=False,
    )
```

```python
import functools
import math

import jax
import jax.numpy as jnp
from jax import lax
from jax.experimental import pallas as pl
from jax.experimental.pallas import tpu as pltpu
from jax.sharding import PartitionSpec as P

NS_ITERS = 3
COEF_A = 3.4445
COEF_B = -4.775
COEF_C = 2.0315
MOMENTUM_DECAY = 0.95
LEARN_RATE = 0.02
EPSILON = 1e-07
DIRECTION_SCALE = 1.0 + MOMENTUM_DECAY
FOLD = MOMENTUM_DECAY * MOMENTUM_DECAY / DIRECTION_SCALE
SEGMENT = 4
PIECES = 3
FIRST_GROUP = 14
TOP_SEGMENTS = 3
SEGMENT_ORDER = (2, 1, 3, 0)

VMEM = pl.BlockSpec(memory_space=pltpu.VMEM)
SMEM = pl.BlockSpec(memory_space=pltpu.SMEM)
HBM = pl.BlockSpec(memory_space=pltpu.HBM)


def folded(part, momentum):
    return (part.astype(jnp.float32) + FOLD * momentum).astype(jnp.bfloat16)


def count_slots(owners_ref, first_ref, slot_ref, counted=lambda: None):
    groups = first_ref.shape[0]
    for group in range(groups):
        first_ref[group] = 0
    for block in range(owners_ref.shape[0]):
        owner = owners_ref[block]
        slot = first_ref[owner]
        slot_ref[block] = slot
        first_ref[owner] = slot + 1
    counted()
    first = jnp.int32(0)
    for group in range(groups):
        after = first + first_ref[group]
        first_ref[group] = first
        first = after


def split_rank(groups, rank):
    return rank & (groups - 1), rank >> (groups.bit_length() - 1)


def fold_kernel(
    groups,
    here_ref,
    owners_hbm,
    part_hbm,
    momentum_hbm,
    out_ref,
    owners_ref,
    first_ref,
    target_ref,
    owned_ref,
    part_ref,
    momentum_ref,
    sems,
):
    blocks, most = part_ref.shape[0], momentum_ref.shape[0]
    per_group = blocks // groups
    copies = [
        pltpu.make_async_copy(source, target, sems.at[index])
        for index, (source, target) in enumerate(
            [(owners_hbm, owners_ref), (part_hbm, part_ref), (momentum_hbm, momentum_ref)]
        )
    ]
    for copy in copies:
        copy.start()
    here = here_ref[0]
    copies[0].wait()
    count_slots(owners_ref, first_ref, target_ref)
    count = jnp.int32(0)
    for block in range(blocks):
        owner, slot = owners_ref[block], target_ref[block]
        mine = owner == here
        count = count + mine.astype(jnp.int32)
        owned_ref[jnp.where(mine, slot, most)] = block
        group, place = split_rank(groups, first_ref[owner] + slot)
        target_ref[block] = ((group - FIRST_GROUP) & (groups - 1)) * per_group + place
    copies[1].wait()
    for block in range(blocks):
        out_ref[target_ref[block]] = part_ref[block]
    copies[2].wait()
    for slot in range(most):

        @pl.when(slot < count)
        def _():
            block = owned_ref[slot]
            out_ref[target_ref[block]] = folded(part_ref[block], momentum_ref[slot])


def sums_kernel(
    groups, here_ref, owners_ref, total_ref, out_ref, first_out_ref, slot_out_ref, first_ref, slot_ref, sems
):
    per_group = total_ref.shape[0]
    copies = [
        pltpu.make_async_copy(source, target, sems.at[index])
        for index, (source, target) in enumerate([(first_ref, first_out_ref), (slot_ref, slot_out_ref)])
    ]
    count_slots(owners_ref, first_ref, slot_ref, copies[1].start)
    copies[0].start()
    value = total_ref[0]
    for target in range(groups):
        out_ref[target] = value
    for place in range(per_group):
        rank = place * groups + here_ref[0]
        owner = jnp.int32(-1)
        for group in range(groups):
            owner = owner + (first_ref[group] <= rank).astype(jnp.int32)
        out_ref[owner] = total_ref[place]
    for copy in copies:
        copy.wait()


def sum_kernel(ring, parts_ref, send_ref, total_ref):
    count, blocks = parts_ref.shape[:2]
    for block in range(blocks):
        total = parts_ref[0, block].astype(jnp.float32)
        for source in range(1, count):
            total = total + parts_ref[source, block].astype(jnp.float32)
        total_ref[block] = total.astype(jnp.bfloat16)
        direction = (DIRECTION_SCALE * total).astype(jnp.bfloat16)
        for target, chip in enumerate(ring):
            if min(chip % SEGMENT, blocks - 1) == block:
                send_ref[target] = direction


def dot_nt(a, b):
    return lax.dot_general(a, b, (((1,), (1,)), ((), ())), preferred_element_type=jnp.float32)


def dot_nn(a, b):
    return jnp.dot(a, b, preferred_element_type=jnp.float32)


def newton_schulz_kernel(first_ref, own_ref, other_ref, out_ref, x_ref, y_ref, gram_ref, poly_ref):
    half, order = own_ref.shape
    kept = out_ref.shape[0]
    x_ref[0:half] = own_ref[...]
    x_ref[half:order] = other_ref[...]
    squares = jnp.zeros((8, order), jnp.float32)
    for ref in (own_ref, other_ref):
        wide = ref[...].astype(jnp.float32)
        squares = squares + jnp.sum((wide * wide).reshape(half // 8, 8, order), axis=0)
    inverse = 1.0 / (jnp.sqrt(jnp.sum(squares)) + EPSILON)
    source_ref, target_ref = x_ref, y_ref
    for iteration in range(NS_ITERS):
        gram = dot_nt(source_ref[...], source_ref[...])
        if iteration == 0:
            gram = gram * (inverse * inverse)
        gram_ref[...] = gram.astype(jnp.bfloat16)
        last = iteration == NS_ITERS - 1
        rows = pl.ds(pl.multiple_of(first_ref[0] * kept, kept), kept) if last else pl.ds(0, order)
        gram = gram_ref[rows]
        poly = (COEF_B * gram.astype(jnp.float32) + COEF_C * dot_nn(gram, gram_ref[...])).astype(jnp.bfloat16)
        if not last:
            poly_ref[...] = poly
            poly = poly_ref[...]
        fresh = COEF_A * source_ref[rows].astype(jnp.float32) + dot_nn(poly, source_ref[...])
        if iteration == 0:
            fresh = fresh * inverse
        if last:
            each = kept // SEGMENT
            for target, chip in enumerate(SEGMENT_ORDER):
                start = (SEGMENT - 1 - chip) * each
                out_ref[target * each : (target + 1) * each] = fresh[start : start + each].astype(jnp.bfloat16)
        else:
            target_ref[...] = fresh.astype(jnp.bfloat16)
            source_ref, target_ref = target_ref, source_ref


def spread_kernel(returned_ref, sums_ref, out_ref):
    per_group = out_ref.shape[1] - 1
    for target in range(out_ref.shape[0]):
        out_ref[target, per_group] = sums_ref[target]
    for place in range(per_group):
        value = returned_ref[SEGMENT_ORDER.index(place)]
        for target in range(out_ref.shape[0]):
            out_ref[target, place] = value


def update_kernel(
    groups,
    scale,
    here_ref,
    owners_ref,
    first_ref,
    slot_ref,
    both_ref,
    weight_ref,
    part_ref,
    momentum_ref,
    step_hbm,
    new_hbm,
    moved_hbm,
    owned_ref,
    step_ref,
    new_ref,
    moved_ref,
    sems,
    moved_sem,
):
    blocks, most = weight_ref.shape[0], momentum_ref.shape[0]
    per_group = blocks // groups
    each = blocks // PIECES
    leaving = []

    def leave(source, target, sem):
        leaving.append(pltpu.make_async_copy(source, target, sem))
        leaving[-1].start()

    for index in range(PIECES):
        chunk = pl.ds(index * each, each)
        for block in range(index * each, (index + 1) * each):
            group, place = split_rank(groups, first_ref[owners_ref[block]] + slot_ref[block])
            step = both_ref[group, place].astype(jnp.float32) * scale
            step_ref[block] = step
            new_ref[block] = weight_ref[block] - LEARN_RATE * step
        leave(step_ref.at[chunk], step_hbm.at[chunk], sems.at[index, 0])
        leave(new_ref.at[chunk], new_hbm.at[chunk], sems.at[index, 1])
    here = here_ref[0]
    first = first_ref[here]
    count = jnp.int32(0)
    for block in range(blocks):
        mine = owners_ref[block] == here
        count = count + mine.astype(jnp.int32)
        owned_ref[jnp.where(mine, slot_ref[block], most)] = block
    for slot in range(most):
        used = slot < count
        block = jnp.where(used, owned_ref[slot], 0)
        group, _ = split_rank(groups, first + slot)
        part = part_ref[block]
        before = momentum_ref[slot]
        added = folded(part, before).astype(jnp.float32) - part.astype(jnp.float32)
        gradient = both_ref[group, per_group].astype(jnp.float32) - added
        moved_ref[slot] = jnp.where(used, MOMENTUM_DECAY * before + gradient, before)
    leave(moved_ref, moved_hbm, moved_sem)
    for copy in leaving:
        copy.wait()


def call(kernel, out_shape, in_specs, scratch=(), flops=0, moved=0, out_specs=None):
    return pl.pallas_call(
        kernel,
        out_shape=out_shape,
        in_specs=in_specs,
        out_specs=jax.tree.map(lambda _: VMEM, out_shape) if out_specs is None else out_specs,
        scratch_shapes=list(scratch),
        compiler_params=pltpu.CompilerParams(vmem_limit_bytes=24 * 1024 * 1024),
        cost_estimate=pl.CostEstimate(flops=flops, bytes_accessed=moved, transcendentals=0),
    )


def on_device(grad_parts, momentum, weight, owners):
    part = grad_parts[0]
    blocks, rows, order = part.shape
    most = momentum.shape[0]
    groups = lax.axis_size("rep")
    members = lax.axis_size("fsdp")
    chips = members // 2
    per_group = blocks // groups
    bf16 = functools.partial(jax.ShapeDtypeStruct, dtype=jnp.bfloat16)
    f32 = functools.partial(jax.ShapeDtypeStruct, dtype=jnp.float32)
    here = lax.axis_index("rep").astype(jnp.int32).reshape(1)
    segments = chips // SEGMENT
    ring = [(SEGMENT * TOP_SEGMENTS - 1 - index) % chips for index in range(chips)]
    same_core = [[2 * chip + core for chip in ring] for core in range(2)]
    same_segment = [
        [2 * (SEGMENT * s + chip) + core for chip in SEGMENT_ORDER] for s in range(segments) for core in range(2)
    ]
    from_first = [[(FIRST_GROUP + index) % groups for index in range(groups)]]
    segment = lax.axis_index("fsdp") // (2 * SEGMENT)
    listed = lax.rem(TOP_SEGMENTS - 1 + segments - segment, segments).astype(jnp.int32).reshape(1)

    with jax.named_scope("fold_momentum"):
        parts = call(
            functools.partial(fold_kernel, groups),
            pltpu.VMEM((blocks, rows, order), jnp.bfloat16),
            [SMEM, HBM, HBM, HBM],
            [
                pltpu.SMEM((blocks,), jnp.int32),
                pltpu.SMEM((groups,), jnp.int32),
                pltpu.SMEM((blocks,), jnp.int32),
                pltpu.SMEM((most + 1,), jnp.int32),
                pltpu.VMEM(part.shape, jnp.bfloat16),
                pltpu.VMEM(momentum.shape, jnp.float32),
                pltpu.SemaphoreType.DMA((3,)),
            ],
            moved=1 << 21,
        )(here, *(pltpu.with_memory_space_constraint(array, pltpu.HBM) for array in (owners, part, momentum)))
    with jax.named_scope("reduce_over_rep"):
        received = lax.all_to_all(
            parts.reshape(groups, per_group, rows, order),
            "rep",
            0,
            0,
            axis_index_groups=from_first,
            tiled=True,
        )
        send, total = call(
            functools.partial(sum_kernel, ring),
            [bf16((chips, rows, order)), bf16((per_group, rows, order))],
            [VMEM],
            moved=1 << 20,
        )(received)
    with jax.named_scope("gather_rows"):
        own = lax.all_to_all(send, "fsdp", 0, 0, axis_index_groups=same_core, tiled=True)
        own = own.reshape(chips * rows, order)
        other = lax.ppermute(own, "fsdp", [(i, i ^ 1) for i in range(members)])
    with jax.named_scope("sums_to_owners"):
        late_owners, own = lax.optimization_barrier((owners, own))
        sums, first, slots = call(
            functools.partial(sums_kernel, groups),
            [
                pltpu.VMEM((groups, rows, order), jnp.bfloat16),
                pltpu.VMEM((groups,), jnp.int32),
                pltpu.VMEM((blocks,), jnp.int32),
            ],
            [SMEM, SMEM, VMEM],
            [
                pltpu.SMEM((groups,), jnp.int32),
                pltpu.SMEM((blocks,), jnp.int32),
                pltpu.SemaphoreType.DMA((2,)),
            ],
            moved=1 << 20,
        )(here, late_owners, total)
        other, slots = lax.optimization_barrier((other, slots))
    with jax.named_scope("orthogonalize"):
        square = pltpu.VMEM((order, order), jnp.bfloat16)
        kept = call(
            newton_schulz_kernel,
            bf16((SEGMENT * rows, order)),
            [SMEM, VMEM, VMEM],
            [square] * 4,
            flops=15 * order**3,
            moved=1 << 20,
        )(listed, own, other)
    with jax.named_scope("return_rows"):
        returned = lax.all_to_all(
            kept.reshape(SEGMENT, rows, order), "fsdp", 0, 0, axis_index_groups=same_segment, tiled=True
        )
        spread = call(
            spread_kernel,
            bf16((groups, per_group + 1, rows, order)),
            [VMEM, VMEM],
            moved=1 << 20,
        )(returned, sums)
        both = lax.all_to_all(spread, "rep", 0, 0, tiled=True)
    with jax.named_scope("update"):
        return call(
            functools.partial(update_kernel, groups, 0.2 * math.sqrt(order)),
            [f32(weight.shape), f32(weight.shape), f32(momentum.shape)],
            [SMEM, SMEM, SMEM, SMEM, VMEM, VMEM, VMEM, VMEM],
            [
                pltpu.SMEM((most + 1,), jnp.int32),
                pltpu.VMEM(weight.shape, jnp.float32),
                pltpu.VMEM(weight.shape, jnp.float32),
                pltpu.VMEM(momentum.shape, jnp.float32),
                pltpu.SemaphoreType.DMA((PIECES, 2)),
                pltpu.SemaphoreType.DMA,
            ],
            moved=5 << 20,
            out_specs=[HBM, HBM, HBM],
        )(here, late_owners, first, slots, both, weight, part, momentum)


def solution(mesh):
    return jax.shard_map(
        on_device,
        mesh=mesh,
        in_specs=(P("rep", None, "fsdp", None), P("rep", "fsdp", None), P(None, "fsdp", None), P()),
        out_specs=(P(None, "fsdp", None), P(None, "fsdp", None), P("rep", "fsdp", None)),
        check_vma=False,
    )
```
